256 devices in a mesh: tile: 32 (over x, z), pair: 8 (over y, core).
Axes of the slice: x: 4, y: 4, z: 8, core: 2. Of those that a mesh axis runs over, the one named last changes fastest.
Arguments:
- amplitudes: float32 [512, 32768], P('pair', 'tile'), may hold values from -6 to 6
- driver: float32 [512, 32768], P('pair', 'tile'), may hold values from -6 to 6
- integrals: float32 [2048, 128, 128], P('tile'), may hold values from -0.25 to 0.25
- tile_rows: int32 [2048], P('tile'), may hold values from 0 to 255, as said below
- tile_cols: int32 [2048], P('tile'), may hold values from 0 to 255, as said below
- tile_count: int32 [32], P('tile'), may hold values from 16 to 64, as said below
- pair_energy: float32 [512], P('pair'), may hold values from -3 to -0.5
- virt_energy: float32 [32768], P('tile'), may hold values from 0.5 to 4
Outputs:
- new_amps: float32 [512, 32768], P('pair', 'tile')
The draws below stay inside these ranges and needn't reach their ends.
Inputs may be any that keep to these rules, and one draw needn't show every extreme that they name: The first tile_count[o] slots of owner o are live; at least one owner has all 64 live. `tile_rows`: with tile_cols, names the row tile of each slot; a slot's row and column tiles lie in one symmetry sector; sector s (s = 0 to 7) is the tiles 4*s*s to 4*(s+1)*(s+1)-1; no (row tile, column tile) pair is named by two slots. `tile_cols`: the column tile of each slot, in the sector of its row tile.
All inputs are finite; a program needn't handle non-finite values.
Results may differ from the reference program's by a relative error of at most 0.0003.
Values sent between devices are 32-bit elements; how exact they have to be, the bound alone decides.
No kernel may reach another device: no remote copies, remote signals or barrier semaphores. Data moves between devices by JAX's collectives and lax.ppermute only.
A program may use at most 128 MiB of HBM per device.

```python
import jax
import jax.numpy as jnp
from jax import lax

TILE_WIDTH = 128
COL_TILES = 8
SLOTS = 64
IRREPS = 8
OWNERS = 32
TILES_ALL = 256
VPAIRS = 32768
PAIRS = 512


def tile_pairs(key):
    tile_total = TILES_ALL
    bounds = [tile_total * step * step // (IRREPS * IRREPS) for step in range(IRREPS + 1)]
    widths = [bounds[step + 1] - bounds[step] for step in range(IRREPS)]
    offsets = [0]
    for width in widths:
        offsets.append(offsets[-1] + width * width)
    pair_total = offsets[-1]
    lower_table = jnp.array(bounds[:IRREPS], dtype=jnp.int32)
    width_table = jnp.array([max(width, 1) for width in widths], dtype=jnp.int32)
    offset_table = jnp.array(offsets, dtype=jnp.int32)
    picked = jax.random.permutation(jax.random.fold_in(key, 11), pair_total)[:OWNERS * SLOTS].astype(jnp.int32)
    sector = jnp.sum((offset_table[None, 1:] <= picked[:, None]).astype(jnp.int32), axis=1)
    local = picked - offset_table[sector]
    width_here = width_table[sector]
    lower = lower_table[sector]
    row_ids = lower + local // width_here
    col_ids = lower + local % width_here
    return (row_ids, col_ids)


def draw_tile_rows(key, part):
    shared = tile_pairs(key)
    return shared[0].astype(jnp.int32)


def draw_tile_cols(key, part):
    shared = tile_pairs(key)
    return shared[1].astype(jnp.int32)


def draw_tile_count(key, part):
    key = jax.random.fold_in(key, 3)
    first = jax.random.randint(jax.random.fold_in(key, 1), (OWNERS,), SLOTS // 4, SLOTS + 1, dtype=jnp.int32)
    second = jax.random.randint(jax.random.fold_in(key, 2), (OWNERS,), SLOTS // 4, SLOTS + 1, dtype=jnp.int32)
    counts = jnp.minimum(first, second)
    fullest = jax.random.randint(jax.random.fold_in(key, 4), (), 0, OWNERS, dtype=jnp.int32)
    counts = jnp.where(jnp.arange(OWNERS, dtype=jnp.int32) == fullest, SLOTS, counts)
    return counts.astype(jnp.int32)


def steps_of(rng, extent, cuts, smallest, largest):
    loudness = 1.0
    for dim, parts in cuts:
        heights = jax.random.uniform(jax.random.fold_in(jax.random.fold_in(rng, 6), dim), (parts,), jnp.float32, smallest / len(cuts), largest / len(cuts))
        loudness = loudness * jnp.repeat(jnp.exp(heights), extent[dim] // parts).reshape((-1,) + (1,) * (len(extent) - 1 - dim))
    return loudness


def centred(rng, shape, deviation, bound, split=(), held_as=jnp.bfloat16):
    factor_of = steps_of(rng, shape, split, -0.22, 0.18) if split else 1.0
    values = jax.random.normal(rng, shape, jnp.float32) * deviation * factor_of
    return jnp.minimum(jnp.maximum(values, -bound), bound).astype(held_as)


def setup_inputs(seed: int = 0) -> dict:
    streams_of = jax.random.split(jax.random.key(seed), 9)
    amplitudes = centred(streams_of[0], (PAIRS, VPAIRS), 1.0, 6.0, ((0, 8), (1, 32)), jnp.float32)
    driver = centred(streams_of[1], (PAIRS, VPAIRS), 1.0, 6.0, ((0, 8), (1, 32)), jnp.float32)
    integrals = centred(streams_of[2], (OWNERS * SLOTS, TILE_WIDTH, TILE_WIDTH), (TILE_WIDTH * SLOTS // COL_TILES // 2) ** -0.5, 0.25, ((0, 32),), jnp.float32)
    tile_rows = draw_tile_rows(jax.random.fold_in(streams_of[8], 71), 0)
    tile_cols = draw_tile_cols(jax.random.fold_in(streams_of[8], 71), 0)
    tile_count = draw_tile_count(jax.random.fold_in(streams_of[8], 71), 0)
    pair_energy = jnp.clip(-3.0 + 2.5 * jax.random.uniform(streams_of[6], (PAIRS,), jnp.float32) ** steps_of(streams_of[6], (PAIRS,), ((0, 8),), -0.2, 0.2), -3.0, -0.5)
    virt_energy = jnp.clip(0.5 + 3.5 * jax.random.uniform(streams_of[7], (VPAIRS,), jnp.float32) ** steps_of(streams_of[7], (VPAIRS,), ((0, 32),), -0.2, 0.2), 0.5, 4.0)
    return dict(amplitudes=amplitudes, driver=driver, integrals=integrals, tile_rows=tile_rows, tile_cols=tile_cols, tile_count=tile_count, pair_energy=pair_energy, virt_energy=virt_energy)


def reference(amplitudes, driver, integrals, tile_rows, tile_cols, tile_count, pair_energy, virt_energy):
    rows_all = amplitudes.shape[0]
    blocks = amplitudes.reshape(rows_all, TILES_ALL, TILE_WIDTH)
    owner_tiles = integrals.reshape(OWNERS, SLOTS, TILE_WIDTH, TILE_WIDTH)
    row_table = tile_rows.reshape(OWNERS, SLOTS)
    col_table = tile_cols.reshape(OWNERS, SLOTS)

    def owner_step(totals, member):
        pieces, row_ids, col_ids, live_count = member
        active = (jnp.arange(SLOTS, dtype=jnp.int32) < live_count).astype(jnp.float32)
        inputs = jnp.take(blocks, row_ids, axis=1)
        product = jnp.einsum("pgk,gkn->pgn", inputs, pieces, precision=lax.Precision.HIGHEST)
        product = product * active[None, :, None]
        return totals.at[:, col_ids, :].add(product), None

    start_totals = jnp.zeros((rows_all, TILES_ALL, TILE_WIDTH), jnp.float32)
    ladder, unused = lax.scan(owner_step, start_totals, (owner_tiles, row_table, col_table, tile_count))
    ladder = ladder.reshape(rows_all, VPAIRS)
    denominator = virt_energy[None, :] - pair_energy[:, None]
    return (driver + ladder) / denominator
```

```python
import jax
import jax.numpy as jnp
from jax import lax
from jax.experimental import pallas as pl
from jax.experimental.pallas import tpu as pltpu
from jax.sharding import PartitionSpec as P

XS = 4
ZS = 8
YS = 4
CAP = 32
TOTAL_CAP = 80
GROUP = 4
EXTRA = 16
HERE = 64
PIECE = 16
WIDTH = 128

Z_GROUPS = [[x * ZS + z for z in range(ZS)] for x in range(XS)]


def x_shift(step):
    return [(x * ZS + z, ((x + step) % XS) * ZS + z) for x in range(XS) for z in range(ZS)]


def z_shift(step):
    return [(x * ZS + z, x * ZS + (z + step) % ZS) for x in range(XS) for z in range(ZS)]


def y_shift(step):
    return [(y * 2 + core, ((y + step) % YS) * 2 + core) for y in range(YS) for core in range(2)]


CORE_SWAP = [(y * 2 + core, y * 2 + 1 - core) for y in range(YS) for core in range(2)]


def contract(blocks, stored, row_list, col_list, live_count):
    tile_width = stored.shape[1]
    group_size = 8
    slot_total = stored.shape[0]
    rows_here = blocks.shape[0]
    groups = (live_count + group_size - 1) // group_size

    def group_step(group, totals):
        index_list = group * group_size + jnp.arange(group_size, dtype=jnp.int32)
        safe_index = jnp.minimum(index_list, slot_total - 1)
        pieces = jnp.take(stored, safe_index, axis=0)
        row_ids = jnp.take(row_list, safe_index, axis=0)
        col_ids = jnp.take(col_list, safe_index, axis=0)
        active = (index_list < live_count).astype(jnp.float32)
        inputs = jnp.take(blocks, row_ids, axis=1)
        product = jnp.einsum("pgk,gkn->pgn", inputs, pieces, precision=lax.Precision.HIGHEST)
        product = product * active[None, :, None]
        return totals.at[:, col_ids, :].add(product)

    start_totals = jnp.zeros((rows_here, blocks.shape[1], tile_width), jnp.float32)
    return lax.fori_loop(0, groups, group_step, start_totals)


def dense_ladder(amplitudes, integrals, tile_rows, tile_cols, tile_count):
    rows_here = amplitudes.shape[0]
    columns_all = amplitudes.shape[1] * lax.axis_size("tile")
    gathered = lax.all_gather(amplitudes, "tile", axis=1, tiled=True)
    blocks = gathered.reshape(rows_here, columns_all // WIDTH, WIDTH)
    partial_value = contract(blocks, integrals, tile_rows, tile_cols, tile_count[0])
    partial_value = partial_value.reshape(rows_here, columns_all)
    return lax.psum_scatter(partial_value, "tile", scatter_dimension=1, tiled=True)


def home(row, col):
    return jnp.minimum(row, col) // HERE


def pack_kernel(place, rows, cols, count, stored, *refs):
    outs, packed = refs[:XS], refs[XS]
    mine = place[0]

    def step(slot, counts):
        target = lax.rem(home(rows[slot], cols[slot]) - mine + XS, XS)
        position = counts[0]
        for j in range(1, XS):
            position = jnp.where(target == j, counts[j], position)

        @pl.when(position < CAP)
        def _():
            packed[target * CAP + position] = stored[slot]

        return tuple(counts[j] + (target == j).astype(jnp.int32) for j in range(XS))

    lax.fori_loop(0, count[0], step, (jnp.int32(0),) * XS)
    for j in range(XS):
        outs[j][...] = packed[j * CAP:(j + 1) * CAP]


def pack(place, rows, cols, count, integrals):
    slots = integrals.shape[0]
    spec = pltpu.PrefetchScalarGridSpec(
        num_scalar_prefetch=4,
        grid=(1,),
        in_specs=[pl.BlockSpec((slots, PIECE, WIDTH), lambda i, place, *_: (0, place[1], 0))],
        out_specs=[pl.BlockSpec((CAP, PIECE, WIDTH), lambda i, *_: (0, 0, 0))] * XS,
        scratch_shapes=[pltpu.VMEM((XS * CAP, PIECE, WIDTH), jnp.float32)],
    )
    return pl.pallas_call(
        pack_kernel,
        grid_spec=spec,
        out_shape=[jax.ShapeDtypeStruct((CAP, PIECE, WIDTH), jnp.float32)] * XS,
        compiler_params=pltpu.CompilerParams(vmem_limit_bytes=16 * 2**20),
        name="pack",
    )(place, rows, cols, count, integrals)


def plan_kernel(place, *refs):
    metas, (row_at, col_at, info) = refs[:XS], refs[XS:]
    mine = place[0]
    low = mine * HERE
    total = jnp.int32(0)
    over = jnp.int32(0)
    for j in range(XS):
        meta = metas[j]
        base = total

        def step(slot, found):
            row, col = meta[0, slot], meta[1, slot]
            wanted = home(row, col) == mine

            @pl.when(wanted & (base + found < TOTAL_CAP))
            def _():
                row_at[base + found] = row - low
                col_at[base + found] = col - low

            return found + wanted.astype(jnp.int32)

        found = lax.fori_loop(0, meta[2, 0], step, jnp.int32(0))
        over = jnp.maximum(over, (found > CAP).astype(jnp.int32))
        info[j] = jnp.minimum(found, CAP)
        total = total + found
    over = jnp.maximum(over, (total > TOTAL_CAP).astype(jnp.int32))
    info[XS] = jnp.minimum(total, TOTAL_CAP)
    info[XS + 1] = over
    for extra in range(GROUP):
        row_at[info[XS] + extra] = 0
        col_at[info[XS] + extra] = HERE + EXTRA
    for rest in range(XS + 2, 8):
        info[rest] = 0


def plan(place, metas):
    smem = pl.BlockSpec(memory_space=pltpu.SMEM)
    return pl.pallas_call(
        plan_kernel,
        in_specs=[smem] * (1 + XS),
        out_specs=[smem] * 3,
        out_shape=[
            jax.ShapeDtypeStruct((TOTAL_CAP + GROUP,), jnp.int32),
            jax.ShapeDtypeStruct((TOTAL_CAP + GROUP,), jnp.int32),
            jax.ShapeDtypeStruct((8,), jnp.int32),
        ],
        name="plan",
    )(place, *metas)


def compact_kernel(info, *refs):
    sources, out = refs[:XS], refs[XS]
    base = jnp.int32(0)
    for j in range(XS):
        source = sources[j]

        def step(item, _):
            @pl.when(base + item < TOTAL_CAP)
            def _():
                out[base + item] = source[item]

            return 0

        lax.fori_loop(0, info[j], step, 0)
        base = base + info[j]


def compact(info, sources):
    vmem = pl.BlockSpec(memory_space=pltpu.VMEM)
    return pl.pallas_call(
        compact_kernel,
        in_specs=[pl.BlockSpec(memory_space=pltpu.SMEM)] + [vmem] * XS,
        out_specs=vmem,
        out_shape=jax.ShapeDtypeStruct((TOTAL_CAP, PIECE, WIDTH), jnp.float32),
        compiler_params=pltpu.CompilerParams(vmem_limit_bytes=16 * 2**20),
        name="compact",
    )(info, *sources)


def ladder_kernel(place, row_at, col_at, info, near, extra, *refs):
    pieces = refs[:2 * YS]
    out, out_extra, split, tile, sums = refs[2 * YS:]
    rows_here = near.shape[1]
    for block in range(ZS + 2):
        for part in range(ZS):
            source = near if block < ZS else extra
            at = block if block < ZS else block - ZS
            value = source[at, :, part * WIDTH:(part + 1) * WIDTH]
            high = value.astype(jnp.bfloat16)
            split[block * ZS + part, :, :WIDTH] = high
            split[block * ZS + part, :, WIDTH:] = (value - high.astype(jnp.float32)).astype(jnp.bfloat16)
    sums[...] = jnp.zeros_like(sums)
    my_y = lax.div(place[1], 2)
    my_core = lax.rem(place[1], 2)
    blank = jnp.zeros((WIDTH, WIDTH), jnp.bfloat16)

    def step(group, _):
        products = []
        for member in range(GROUP):
            item = group * GROUP + member
            safe = jnp.minimum(item, TOTAL_CAP - 1)
            for shift in range(YS):
                for swapped in range(2):
                    core = my_core if swapped == 0 else 1 - my_core
                    origin = lax.rem(my_y - shift + YS, YS) * 2 + core
                    at = pl.multiple_of(origin * PIECE, PIECE)
                    tile[member, pl.ds(at, PIECE), :] = pieces[shift * 2 + swapped][safe]
            value = tile[member]
            high = value.astype(jnp.bfloat16)
            low = (value - high.astype(jnp.float32)).astype(jnp.bfloat16)
            right = jnp.concatenate(
                [jnp.concatenate([high, low], axis=1), jnp.concatenate([high, blank], axis=1)], axis=0
            )
            product = jnp.dot(split[row_at[item]], right, preferred_element_type=jnp.float32)
            products.append(product[:, :WIDTH] + product[:, WIDTH:])
        for member in range(GROUP):
            item = group * GROUP + member
            sums[col_at[item]] += products[member]
        return 0

    groups = lax.div(info[XS] + GROUP - 1, GROUP)
    lax.fori_loop(0, groups, step, 0)
    for block in range(ZS):
        for part in range(ZS):
            out[block, :, part * WIDTH:(part + 1) * WIDTH] = sums[block * ZS + part]
    for block in range(2):
        for part in range(ZS):
            out_extra[block, :, part * WIDTH:(part + 1) * WIDTH] = sums[HERE + block * ZS + part]


def ladder_of(place, row_at, col_at, info, near, extra, pieces):
    rows_here = near.shape[1]
    wide = near.shape[2]
    vmem = pl.BlockSpec(memory_space=pltpu.VMEM)
    smem = pl.BlockSpec(memory_space=pltpu.SMEM)
    return pl.pallas_call(
        ladder_kernel,
        in_specs=[smem] * 4 + [vmem] * (2 + 2 * YS),
        out_specs=[vmem, vmem],
        out_shape=[
            jax.ShapeDtypeStruct((ZS, rows_here, wide), jnp.float32),
            jax.ShapeDtypeStruct((2, rows_here, wide), jnp.float32),
        ],
        scratch_shapes=[
            pltpu.VMEM((HERE + EXTRA, rows_here, 2 * WIDTH), jnp.bfloat16),
            pltpu.VMEM((GROUP, WIDTH, WIDTH), jnp.float32),
            pltpu.VMEM((HERE + EXTRA + 1, rows_here, WIDTH), jnp.float32),
        ],
        compiler_params=pltpu.CompilerParams(vmem_limit_bytes=40 * 2**20),
        name="ladder",
    )(place, row_at, col_at, info, near, extra, *pieces)


def shards(
    amplitudes, driver, integrals, tile_rows, tile_cols, tile_count, pair_energy, virt_energy
):
    my_tile = lax.axis_index("tile")
    my_x = my_tile // ZS
    my_pair = lax.axis_index("pair")
    place = jnp.stack([my_x, my_pair]).astype(jnp.int32)

    near = lax.all_gather(amplitudes, "tile", axis=0, axis_index_groups=Z_GROUPS)
    extra = lax.ppermute(near[:2], "tile", x_shift(-1))

    meta = jnp.stack([tile_rows, tile_cols, jnp.broadcast_to(tile_count, tile_rows.shape)])
    metas = [meta] + [lax.ppermute(meta, "tile", x_shift(step)) for step in range(1, XS)]
    row_at, col_at, info = plan(place, metas)

    packed = pack(place, tile_rows, tile_cols, tile_count, integrals)
    moved = [packed[0]] + [lax.ppermute(packed[step], "tile", x_shift(step)) for step in range(1, XS)]
    mine = compact(info, moved)
    along_y = [mine] + [lax.ppermute(mine, "pair", y_shift(step)) for step in range(1, YS)]
    pieces = []
    for piece in along_y:
        pieces += [piece, lax.ppermute(piece, "pair", CORE_SWAP)]

    out, out_extra = ladder_of(place, row_at, col_at, info, near, extra, pieces)
    from_left = lax.ppermute(out_extra, "tile", x_shift(1))
    from_left = jnp.where(my_x > 0, from_left, 0.0)
    out = jnp.concatenate([out[:2] + from_left, out[2:]], axis=0)
    quick = lax.psum_scatter(out, "tile", scatter_dimension=0, axis_index_groups=Z_GROUPS, tiled=True)[0]

    over = info[XS + 1:XS + 2].astype(jnp.float32)
    for step in (1, 2):
        over = jnp.maximum(over, lax.ppermute(over, "tile", x_shift(step)))
    for step in (1, 2, 4):
        over = jnp.maximum(over, lax.ppermute(over, "tile", z_shift(step)))

    denominator = virt_energy[None, :] - pair_energy[:, None]
    result = (driver + quick) / denominator

    def slow():
        ladder = dense_ladder(amplitudes, integrals, tile_rows, tile_cols, tile_count)
        return (driver + ladder) / denominator

    return lax.cond(over[0] > 0.5, slow, lambda: result)


def solution(mesh):
    return jax.shard_map(
        shards,
        mesh=mesh,
        in_specs=(
            P("pair", "tile"),
            P("pair", "tile"),
            P("tile", None, None),
            P("tile"),
            P("tile"),
            P("tile"),
            P("pair"),
            P("tile"),
        ),
        out_specs=P("pair", "tile"),
        check_vma=False,
    )
```

```python
import jax
import jax.numpy as jnp
from jax import lax
from jax.experimental import pallas as pl
from jax.experimental.pallas import tpu as pltpu
from jax.sharding import PartitionSpec as P

XS = 4
ZS = 8
YS = 4
CAP = 32
TOTAL_CAP = 68
SLOTS = 64
GROUP = 4
EXTRA = 16
HERE = 64
PIECE = 16
WIDTH = 128

Z_GROUPS = [[x * ZS + z for z in range(ZS)] for x in range(XS)]


def x_shift(step):
    return [(x * ZS + z, ((x + step) % XS) * ZS + z) for x in range(XS) for z in range(ZS)]


def z_shift(step):
    return [(x * ZS + z, x * ZS + (z + step) % ZS) for x in range(XS) for z in range(ZS)]


def y_shift(step):
    return [(y * 2 + core, ((y + step) % YS) * 2 + core) for y in range(YS) for core in range(2)]


CORE_SWAP = [(y * 2 + core, y * 2 + 1 - core) for y in range(YS) for core in range(2)]


def contract(blocks, stored, row_list, col_list, live_count):
    tile_width = stored.shape[1]
    group_size = 8
    slot_total = stored.shape[0]
    rows_here = blocks.shape[0]
    groups = (live_count + group_size - 1) // group_size

    def group_step(group, totals):
        index_list = group * group_size + jnp.arange(group_size, dtype=jnp.int32)
        safe_index = jnp.minimum(index_list, slot_total - 1)
        pieces = jnp.take(stored, safe_index, axis=0)
        row_ids = jnp.take(row_list, safe_index, axis=0)
        col_ids = jnp.take(col_list, safe_index, axis=0)
        active = (index_list < live_count).astype(jnp.float32)
        inputs = jnp.take(blocks, row_ids, axis=1)
        product = jnp.einsum("pgk,gkn->pgn", inputs, pieces, precision=lax.Precision.HIGHEST)
        product = product * active[None, :, None]
        return totals.at[:, col_ids, :].add(product)

    start_totals = jnp.zeros((rows_here, blocks.shape[1], tile_width), jnp.float32)
    return lax.fori_loop(0, groups, group_step, start_totals)


def dense_ladder(amplitudes, integrals, tile_rows, tile_cols, tile_count):
    rows_here = amplitudes.shape[0]
    columns_all = amplitudes.shape[1] * lax.axis_size("tile")
    gathered = lax.all_gather(amplitudes, "tile", axis=1, tiled=True)
    blocks = gathered.reshape(rows_here, columns_all // WIDTH, WIDTH)
    partial_value = contract(blocks, integrals, tile_rows, tile_cols, tile_count[0])
    partial_value = partial_value.reshape(rows_here, columns_all)
    return lax.psum_scatter(partial_value, "tile", scatter_dimension=1, tiled=True)


def home(row, col):
    return jnp.minimum(row, col) // HERE


def pack_kernel(place, rows, cols, count, stored, *refs):
    outs, own, sizes, packed = refs[:XS - 1], refs[XS - 1], refs[XS], refs[XS + 1]
    mine = place[0]
    low = mine * HERE
    lane = lax.broadcasted_iota(jnp.int32, (PIECE, WIDTH), 1)
    line = lax.broadcasted_iota(jnp.int32, (PIECE, WIDTH), 0)
    for j in range(1, XS):
        packed[j * (CAP + 1) + CAP] = jnp.full((PIECE, WIDTH), -1.0, jnp.float32)

    def step(slot, counts):
        row, col = rows[slot], cols[slot]
        target = lax.rem(home(row, col) - mine + XS, XS)
        outside = (target == 0) & (col - low >= HERE)
        position = jnp.int32(0)
        for j in range(1, XS):
            position = jnp.where(target == j, counts[j], position)

        @pl.when((target > 0) & (position < CAP))
        def _():
            packed[target * (CAP + 1) + position] = stored[slot]
            at = target * (CAP + 1) + CAP
            entry = jnp.where(line == 0, row, col).astype(jnp.float32)
            packed[at] = jnp.where((lane == position) & (line < 2), entry, packed[at])

        @pl.when(outside)
        def _():
            at = counts[XS]
            own[0, at] = slot
            own[1, at] = row - low
            own[2, at] = col - low

        @pl.when((target == 0) & jnp.logical_not(outside))
        def _():
            at = counts[0]
            own[3, at] = slot
            own[4, at] = row - low
            own[5, at] = col - low

        hits = [(target == j).astype(jnp.int32) for j in range(XS)]
        far = outside.astype(jnp.int32)
        return (counts[0] + hits[0] - far,) + tuple(counts[j] + hits[j] for j in range(1, XS)) + (counts[XS] + far,)

    counts = lax.fori_loop(0, count[0], step, (jnp.int32(0),) * (XS + 1))
    most = counts[1]
    for j in range(2, XS):
        most = jnp.maximum(most, counts[j])
    over = (most > CAP).astype(jnp.float32)
    sizes[0] = counts[XS]
    sizes[1] = counts[0]
    sizes[2] = (most > CAP).astype(jnp.int32)
    for rest in range(3, 8):
        sizes[rest] = 0
    for list_at, size in ((0, counts[XS]), (3, counts[0])):
        for pad in range(GROUP):
            own[list_at, size + pad] = 0
            own[list_at + 1, size + pad] = 0
            own[list_at + 2, size + pad] = HERE + EXTRA
    for j in range(1, XS):
        at = j * (CAP + 1) + CAP
        packed[at] = jnp.where(line == 2, over, packed[at])
        outs[j - 1][...] = packed[j * (CAP + 1):(j + 1) * (CAP + 1)]


def pack(place, rows, cols, count, integrals):
    slots = integrals.shape[0]
    spec = pltpu.PrefetchScalarGridSpec(
        num_scalar_prefetch=4,
        grid=(1,),
        in_specs=[pl.BlockSpec((slots, PIECE, WIDTH), lambda i, place, *_: (0, place[1], 0))],
        out_specs=[pl.BlockSpec((CAP + 1, PIECE, WIDTH), lambda i, *_: (0, 0, 0))] * (XS - 1)
        + [pl.BlockSpec(memory_space=pltpu.SMEM)] * 2,
        scratch_shapes=[pltpu.VMEM((XS * (CAP + 1), PIECE, WIDTH), jnp.float32)],
    )
    return pl.pallas_call(
        pack_kernel,
        grid_spec=spec,
        out_shape=[jax.ShapeDtypeStruct((CAP + 1, PIECE, WIDTH), jnp.float32)] * (XS - 1)
        + [jax.ShapeDtypeStruct((6, SLOTS + GROUP), jnp.int32), jax.ShapeDtypeStruct((8,), jnp.int32)],
        compiler_params=pltpu.CompilerParams(vmem_limit_bytes=8 * 2**20),
        name="pack",
    )(place, rows, cols, count, integrals)


def compact_kernel(place, sizes, *refs):
    sources, (out, moved, totals, entries, sems) = refs[:XS - 1], refs[XS - 1:]
    low = place[0] * HERE
    copies = [
        pltpu.make_async_copy(sources[j].at[CAP, pl.ds(0, 8)], entries.at[j], sems.at[j]) for j in range(XS - 1)
    ]
    for copy in copies:
        copy.start()
    for copy in copies:
        copy.wait()
    total = jnp.int32(0)
    near = jnp.int32(0)
    far = jnp.int32(0)
    over = sizes[2] > 0
    for j in range(XS - 1):
        source = sources[j]
        over = over | (entries[j, 2, 0] > 0.5)

        def step(item, carry):
            total, near, far = carry
            row = entries[j, 0, item].astype(jnp.int32)
            col = entries[j, 1, item].astype(jnp.int32)
            live = row >= 0
            fits = live & (total < TOTAL_CAP)
            outside = col - low >= HERE

            @pl.when(fits)
            def _():
                out[total] = source[item]

            @pl.when(fits & outside)
            def _():
                moved[0, far] = total
                moved[1, far] = row - low
                moved[2, far] = col - low

            @pl.when(fits & jnp.logical_not(outside))
            def _():
                moved[3, near] = total
                moved[4, near] = row - low
                moved[5, near] = col - low

            return (
                total + live.astype(jnp.int32),
                near + (fits & jnp.logical_not(outside)).astype(jnp.int32),
                far + (fits & outside).astype(jnp.int32),
            )

        total, near, far = lax.fori_loop(0, CAP, step, (total, near, far))
    over = over | (total > TOTAL_CAP)
    totals[0] = far
    totals[1] = near
    totals[2] = over.astype(jnp.int32)
    for rest in range(3, 8):
        totals[rest] = 0
    for list_at, size in ((0, far), (3, near)):
        for pad in range(GROUP):
            moved[list_at, size + pad] = 0
            moved[list_at + 1, size + pad] = 0
            moved[list_at + 2, size + pad] = HERE + EXTRA


def compact(place, sizes, sources):
    vmem = pl.BlockSpec(memory_space=pltpu.VMEM)
    smem = pl.BlockSpec(memory_space=pltpu.SMEM)
    return pl.pallas_call(
        compact_kernel,
        in_specs=[smem] * 2 + [vmem] * (XS - 1),
        out_specs=[vmem, smem, smem],
        out_shape=[
            jax.ShapeDtypeStruct((TOTAL_CAP, PIECE, WIDTH), jnp.float32),
            jax.ShapeDtypeStruct((6, TOTAL_CAP + GROUP), jnp.int32),
            jax.ShapeDtypeStruct((8,), jnp.int32),
        ],
        scratch_shapes=[pltpu.SMEM((XS - 1, 8, WIDTH), jnp.float32), pltpu.SemaphoreType.DMA((XS - 1,))],
        compiler_params=pltpu.CompilerParams(vmem_limit_bytes=8 * 2**20),
        name="compact",
    )(place, sizes, *sources)


def split_of(value):
    high = value.astype(jnp.bfloat16)
    return high, (value - high.astype(jnp.float32)).astype(jnp.bfloat16)


def products_of(place, lists, list_at, size, fetch, split, sums):
    blank = jnp.zeros((WIDTH, WIDTH), jnp.bfloat16)

    def step(group, _):
        products = []
        for member in range(GROUP):
            item = group * GROUP + member
            high, low = split_of(fetch(member, lists[list_at, item]))
            right = jnp.concatenate(
                [jnp.concatenate([high, low], axis=1), jnp.concatenate([high, blank], axis=1)], axis=0
            )
            product = jnp.dot(split[lists[list_at + 1, item]], right, preferred_element_type=jnp.float32)
            products.append(product[:, :WIDTH] + product[:, WIDTH:])
        for member in range(GROUP):
            sums[lists[list_at + 2, group * GROUP + member]] += products[member]
        return 0

    lax.fori_loop(0, lax.div(size + GROUP - 1, GROUP), step, 0)


def fill_split(split, source, first):
    for block in range(source.shape[0]):
        for part in range(ZS):
            high, low = split_of(source[block, :, part * WIDTH:(part + 1) * WIDTH])
            split[first + block * ZS + part, :, :WIDTH] = high
            split[first + block * ZS + part, :, WIDTH:] = low


def fetchers(place, stored, pieces, tile):
    my_y = lax.div(place[1], 2)
    my_core = lax.rem(place[1], 2)

    def own(member, index):
        return stored[index]

    def moved(member, index):
        for shift in range(YS):
            for swapped in range(2):
                core = my_core if swapped == 0 else 1 - my_core
                origin = lax.rem(my_y - shift + YS, YS) * 2 + core
                at = pl.multiple_of(origin * PIECE, PIECE)
                tile[member, pl.ds(at, PIECE), :] = pieces[shift * 2 + swapped][index]
        return tile[member]

    return own, moved


def outer_kernel(place, own, sizes, moved, totals, near, stored, *refs):
    pieces, (out, split, tile, sums) = refs[:2 * YS], refs[2 * YS:]

    @pl.when(sizes[0] + totals[0] > 0)
    def _():
        fill_split(split, near, 0)

    sums[...] = jnp.zeros_like(sums)
    fetch_own, fetch_moved = fetchers(place, stored, pieces, tile)
    products_of(place, own, 0, sizes[0], fetch_own, split, sums)
    products_of(place, moved, 0, totals[0], fetch_moved, split, sums)
    for block in range(2):
        for part in range(ZS):
            out[block, :, part * WIDTH:(part + 1) * WIDTH] = sums[HERE + block * ZS + part]


def inner_kernel(place, own, sizes, moved, totals, marks, near, extra, stored, *refs):
    pieces, outs, (split, tile, sums) = refs[:2 * YS], refs[2 * YS:2 * YS + ZS + 1], refs[2 * YS + ZS + 1:]
    fill_split(split, near, 0)
    fill_split(split, extra, HERE)
    sums[...] = jnp.zeros_like(sums)
    fetch_own, fetch_moved = fetchers(place, stored, pieces, tile)
    products_of(place, own, 3, sizes[1], fetch_own, split, sums)
    products_of(place, moved, 3, totals[1], fetch_moved, split, sums)
    mark = jnp.where(marks[0] > 0.5, jnp.float32(jnp.nan), jnp.float32(0.0))
    half = near.shape[1] // 2
    for step in range(ZS):
        block = lax.rem(place[2] + step, ZS)
        for part in range(ZS):
            value = sums[block * ZS + part] + mark
            lanes = slice(part * WIDTH, (part + 1) * WIDTH)
            if step == ZS // 2:
                outs[step][:, lanes] = value[:half]
                outs[ZS][:, lanes] = value[half:]
            else:
                outs[step][:, lanes] = value


def scratch_of(rows_here):
    return [
        pltpu.VMEM((HERE + EXTRA, rows_here, 2 * WIDTH), jnp.bfloat16),
        pltpu.VMEM((GROUP, WIDTH, WIDTH), jnp.float32),
        pltpu.VMEM((HERE + EXTRA + 1, rows_here, WIDTH), jnp.float32),
    ]


def outer_sums(place, own, sizes, moved, totals, near, stored, pieces):
    _, rows_here, wide = near.shape
    vmem = pl.BlockSpec(memory_space=pltpu.VMEM)
    smem = pl.BlockSpec(memory_space=pltpu.SMEM)
    return pl.pallas_call(
        outer_kernel,
        in_specs=[smem] * 5 + [vmem] * (2 + 2 * YS),
        out_specs=vmem,
        out_shape=jax.ShapeDtypeStruct((2, rows_here, wide), jnp.float32),
        scratch_shapes=scratch_of(rows_here),
        compiler_params=pltpu.CompilerParams(vmem_limit_bytes=12 * 2**20),
        name="outer",
    )(place, own, sizes, moved, totals, near, stored, *pieces)


def inner_sums(place, own, sizes, moved, totals, marks, near, extra, stored, pieces):
    _, rows_here, wide = near.shape
    vmem = pl.BlockSpec(memory_space=pltpu.VMEM)
    smem = pl.BlockSpec(memory_space=pltpu.SMEM)
    heights = [rows_here] * (ZS // 2) + [rows_here // 2] + [rows_here] * (ZS // 2 - 1) + [rows_here // 2]
    return pl.pallas_call(
        inner_kernel,
        in_specs=[smem] * 6 + [vmem] * (3 + 2 * YS),
        out_specs=[vmem] * (ZS + 1),
        out_shape=[jax.ShapeDtypeStruct((height, wide), jnp.float32) for height in heights],
        scratch_shapes=scratch_of(rows_here),
        compiler_params=pltpu.CompilerParams(vmem_limit_bytes=12 * 2**20),
        name="inner",
    )(place, own, sizes, moved, totals, marks, near, extra, stored, *pieces)


def ring_sum(parts, more):
    half = ZS // 2
    rows_here = parts[0].shape[0]
    middle = more(half)
    up = lax.ppermute(parts[half] + middle[:rows_here // 2], "tile", z_shift(1))
    down = lax.ppermute(parts[ZS] + middle[rows_here // 2:], "tile", z_shift(-1))
    up = jnp.concatenate([up, jnp.zeros_like(up)], axis=0)
    down = jnp.concatenate([jnp.zeros_like(down), down], axis=0)
    for step in range(half - 1, 0, -1):
        up = lax.ppermute(up + parts[step] + more(step), "tile", z_shift(1))
        down = lax.ppermute(down + parts[ZS - step] + more(ZS - step), "tile", z_shift(-1))
    return parts[0] + more(0) + up + down


def shards(
    amplitudes, driver, integrals, tile_rows, tile_cols, tile_count, pair_energy, virt_energy
):
    my_tile = lax.axis_index("tile")
    my_x = my_tile // ZS
    my_z = lax.rem(my_tile, ZS)
    place = jnp.stack([my_x, lax.axis_index("pair"), my_z]).astype(jnp.int32)

    near = lax.all_gather(amplitudes, "tile", axis=0, axis_index_groups=Z_GROUPS)
    extra = lax.ppermute(near[:2], "tile", x_shift(-1))

    *packed, own, sizes = pack(place, tile_rows, tile_cols, tile_count, integrals)
    arrived = [lax.ppermute(packed[step - 1], "tile", x_shift(step)) for step in range(1, XS)]
    mine, moved, totals = compact(place, sizes, arrived)
    along_y = [mine] + [lax.ppermute(mine, "pair", y_shift(step)) for step in range(1, YS)]
    pieces = []
    for piece in along_y:
        pieces += [piece, lax.ppermute(piece, "pair", CORE_SWAP)]

    marks = totals[2:3].astype(jnp.float32)
    for step in (1, 2):
        marks = jnp.maximum(marks, lax.ppermute(marks, "tile", x_shift(step)))

    beyond = outer_sums(place, own, sizes, moved, totals, near, integrals, pieces)
    from_left = lax.ppermute(beyond, "tile", x_shift(1))
    from_left = jnp.where(my_x > 0, from_left, 0.0)
    parts = inner_sums(place, own, sizes, moved, totals, marks, near, extra, integrals, pieces)

    def more(step):
        block = lax.rem(my_z + step, ZS)
        return jnp.where(block == 0, from_left[0], jnp.where(block == 1, from_left[1], 0.0))

    ladder = ring_sum(parts, more)
    denominator = virt_energy[None, :] - pair_energy[:, None]
    result = (driver + ladder) / denominator

    def slow():
        full = dense_ladder(amplitudes, integrals, tile_rows, tile_cols, tile_count)
        return (driver + full) / denominator

    return lax.cond(jnp.isnan(ladder[0, 0]), slow, lambda: result)


def solution(mesh):
    return jax.shard_map(
        shards,
        mesh=mesh,
        in_specs=(
            P("pair", "tile"),
            P("pair", "tile"),
            P("tile", None, None),
            P("tile"),
            P("tile"),
            P("tile"),
            P("pair"),
            P("tile"),
        ),
        out_specs=P("pair", "tile"),
        check_vma=False,
    )
```

```python
import jax
import jax.numpy as jnp
from jax import lax
from jax.experimental import pallas as pl
from jax.experimental.pallas import tpu as pltpu
from jax.sharding import PartitionSpec as P

XS = 4
ZS = 8
YS = 4
CAP = 32
TOTAL_CAP = 68
LIST = 72
GROUP = 4
EXTRA = 16
HERE = 64
PIECE = 16
WIDTH = 128

Z_GROUPS = [[x * ZS + z for z in range(ZS)] for x in range(XS)]


def x_shift(step):
    return [(x * ZS + z, ((x + step) % XS) * ZS + z) for x in range(XS) for z in range(ZS)]


def z_shift(step):
    return [(x * ZS + z, x * ZS + (z + step) % ZS) for x in range(XS) for z in range(ZS)]


def y_shift(step):
    return [(y * 2 + core, ((y + step) % YS) * 2 + core) for y in range(YS) for core in range(2)]


CORE_SWAP = [(y * 2 + core, y * 2 + 1 - core) for y in range(YS) for core in range(2)]


def contract(blocks, stored, row_list, col_list, live_count):
    tile_width = stored.shape[1]
    group_size = 8
    slot_total = stored.shape[0]
    rows_here = blocks.shape[0]
    groups = (live_count + group_size - 1) // group_size

    def group_step(group, totals):
        index_list = group * group_size + jnp.arange(group_size, dtype=jnp.int32)
        safe_index = jnp.minimum(index_list, slot_total - 1)
        pieces = jnp.take(stored, safe_index, axis=0)
        row_ids = jnp.take(row_list, safe_index, axis=0)
        col_ids = jnp.take(col_list, safe_index, axis=0)
        active = (index_list < live_count).astype(jnp.float32)
        inputs = jnp.take(blocks, row_ids, axis=1)
        product = jnp.einsum("pgk,gkn->pgn", inputs, pieces, precision=lax.Precision.HIGHEST)
        product = product * active[None, :, None]
        return totals.at[:, col_ids, :].add(product)

    start_totals = jnp.zeros((rows_here, blocks.shape[1], tile_width), jnp.float32)
    return lax.fori_loop(0, groups, group_step, start_totals)


def dense_ladder(amplitudes, integrals, tile_rows, tile_cols, tile_count):
    rows_here = amplitudes.shape[0]
    columns_all = amplitudes.shape[1] * lax.axis_size("tile")
    gathered = lax.all_gather(amplitudes, "tile", axis=1, tiled=True)
    blocks = gathered.reshape(rows_here, columns_all // WIDTH, WIDTH)
    partial_value = contract(blocks, integrals, tile_rows, tile_cols, tile_count[0])
    partial_value = partial_value.reshape(rows_here, columns_all)
    return lax.psum_scatter(partial_value, "tile", scatter_dimension=1, tiled=True)


def home(row, col):
    return jnp.minimum(row, col) // HERE


def pad_list(table, first, size, low):
    for pad in range(GROUP):
        table[0, first + size + pad] = 0
        table[1, first + size + pad] = low
        table[2, first + size + pad] = low + HERE + EXTRA


def pack_kernel(place, rows, cols, count, stored, *refs):
    outs, table, sizes, entries, sems = refs[:XS - 1], refs[XS - 1], refs[XS], refs[XS + 1], refs[XS + 2]
    mine = place[0]
    low = mine * HERE
    for each in range(8):
        sizes[each] = 0

    def sort_step(slot, _):
        row, col = rows[slot], cols[slot]
        target = lax.rem(home(row, col) - mine + XS, XS)
        kind = jnp.where(target == 0, jnp.where(col - low >= HERE, 0, XS), target)
        position = sizes[kind]
        at = kind * LIST + position
        table[0, at] = slot
        table[1, at] = row
        table[2, at] = col
        sizes[kind] = position + 1
        return 0

    lax.fori_loop(0, count[0], sort_step, 0)
    over = jnp.int32(0)
    for j in range(1, XS):
        over = jnp.maximum(over, (sizes[j] > CAP).astype(jnp.int32))
    sizes[XS + 1] = over
    pad_list(table, 0, sizes[0], low)
    pad_list(table, XS * LIST, sizes[XS], low)
    copies = []
    for j in range(1, XS):
        out = outs[j - 1]
        entries[j - 1, 2, 0] = over.astype(jnp.float32)
        entries[j - 1, 3, mine] = 0.0
        for other in range(1, XS):
            entries[j - 1, 3, lax.rem(mine + other, XS)] = sizes[other].astype(jnp.float32)

        def move_step(item, _):
            at = j * LIST + item
            out[item] = stored[table[0, at]]
            entries[j - 1, 0, item] = table[1, at].astype(jnp.float32)
            entries[j - 1, 1, item] = table[2, at].astype(jnp.float32)
            return 0

        lax.fori_loop(0, jnp.minimum(sizes[j], CAP), move_step, 0)
        copy = pltpu.make_async_copy(entries.at[j - 1], out.at[CAP, pl.ds(0, 8)], sems.at[j - 1])
        copy.start()
        copies.append(copy)
    for copy in copies:
        copy.wait()


def pack(place, rows, cols, count, integrals):
    slots = integrals.shape[0]
    spec = pltpu.PrefetchScalarGridSpec(
        num_scalar_prefetch=4,
        grid=(1,),
        in_specs=[pl.BlockSpec((slots, PIECE, WIDTH), lambda i, place, *_: (0, place[1], 0))],
        out_specs=[pl.BlockSpec((CAP + 1, PIECE, WIDTH), lambda i, *_: (0, 0, 0))] * (XS - 1)
        + [pl.BlockSpec(memory_space=pltpu.SMEM)] * 2,
        scratch_shapes=[pltpu.SMEM((XS - 1, 8, WIDTH), jnp.float32), pltpu.SemaphoreType.DMA((XS - 1,))],
    )
    return pl.pallas_call(
        pack_kernel,
        grid_spec=spec,
        out_shape=[jax.ShapeDtypeStruct((CAP + 1, PIECE, WIDTH), jnp.float32)] * (XS - 1)
        + [jax.ShapeDtypeStruct((3, (XS + 1) * LIST), jnp.int32), jax.ShapeDtypeStruct((8,), jnp.int32)],
        compiler_params=pltpu.CompilerParams(vmem_limit_bytes=8 * 2**20),
        name="pack",
    )(place, rows, cols, count, integrals)


def compact_kernel(place, sizes, *refs):
    sources, (out, table, totals, entries, sems) = refs[:XS - 1], refs[XS - 1:]
    mine = place[0]
    low = mine * HERE
    copies = [
        pltpu.make_async_copy(sources[j].at[CAP, pl.ds(0, 8)], entries.at[j], sems.at[j]) for j in range(XS - 1)
    ]
    for copy in copies:
        copy.start()
    for copy in copies:
        copy.wait()
    for each in range(8):
        totals[each] = 0
    over = sizes[XS + 1] > 0
    for j in range(XS - 1):
        over = over | (entries[j, 2, 0] > 0.5)
    for j in range(XS):
        there = lax.rem(mine + j, XS)
        total = jnp.int32(0) if j == 0 else sizes[j]
        for source in range(XS - 1):
            total = total + entries[source, 3, there].astype(jnp.int32)
        over = over | (total > TOTAL_CAP)
    base = jnp.int32(0)
    for j in range(XS - 1):
        source = sources[j]
        size = jnp.minimum(jnp.minimum(entries[j, 3, mine].astype(jnp.int32), CAP), TOTAL_CAP - base)

        def step(item, _):
            row = entries[j, 0, item].astype(jnp.int32)
            col = entries[j, 1, item].astype(jnp.int32)
            out[base + item] = source[item]
            kind = jnp.where(col - low >= HERE, 0, 1)
            position = totals[kind]
            at = kind * LIST + position
            table[0, at] = base + item
            table[1, at] = row
            table[2, at] = col
            totals[kind] = position + 1
            return 0

        lax.fori_loop(0, size, step, 0)
        base = base + size
    totals[2] = over.astype(jnp.int32)
    pad_list(table, 0, totals[0], low)
    pad_list(table, LIST, totals[1], low)


def compact(place, sizes, sources):
    vmem = pl.BlockSpec(memory_space=pltpu.VMEM)
    smem = pl.BlockSpec(memory_space=pltpu.SMEM)
    return pl.pallas_call(
        compact_kernel,
        in_specs=[smem] * 2 + [vmem] * (XS - 1),
        out_specs=[vmem, smem, smem],
        out_shape=[
            jax.ShapeDtypeStruct((TOTAL_CAP, PIECE, WIDTH), jnp.float32),
            jax.ShapeDtypeStruct((3, 2 * LIST), jnp.int32),
            jax.ShapeDtypeStruct((8,), jnp.int32),
        ],
        scratch_shapes=[pltpu.SMEM((XS - 1, 8, WIDTH), jnp.float32), pltpu.SemaphoreType.DMA((XS - 1,))],
        compiler_params=pltpu.CompilerParams(vmem_limit_bytes=8 * 2**20),
        name="compact",
    )(place, sizes, *sources)


def split_of(value):
    high = value.astype(jnp.bfloat16)
    return high, (value - high.astype(jnp.float32)).astype(jnp.bfloat16)


def products_of(low_tile, table, first, size, fetch, split, sums):
    blank = jnp.zeros((WIDTH, WIDTH), jnp.bfloat16)

    def step(group, _):
        products = []
        for member in range(GROUP):
            at = first + group * GROUP + member
            high, low = split_of(fetch(member, table[0, at]))
            right = jnp.concatenate(
                [jnp.concatenate([high, low], axis=1), jnp.concatenate([high, blank], axis=1)], axis=0
            )
            product = jnp.dot(split[table[1, at] - low_tile], right, preferred_element_type=jnp.float32)
            products.append(product[:, :WIDTH] + product[:, WIDTH:])
        for member in range(GROUP):
            col = table[2, first + group * GROUP + member] - low_tile
            lanes = pl.ds(pl.multiple_of(lax.rem(col, ZS) * WIDTH, WIDTH), WIDTH)
            sums[lax.div(col, ZS), :, lanes] += products[member]
        return 0

    lax.fori_loop(0, lax.div(size + GROUP - 1, GROUP), step, 0)


def fill_split(split, source, first):
    for block in range(source.shape[0]):
        for part in range(ZS):
            high, low = split_of(source[block, :, part * WIDTH:(part + 1) * WIDTH])
            split[first + block * ZS + part, :, :WIDTH] = high
            split[first + block * ZS + part, :, WIDTH:] = low


def fetchers(place, stored, pieces, tile):
    my_y = lax.div(place[1], 2)
    my_core = lax.rem(place[1], 2)

    def own(member, index):
        return stored[index]

    def moved(member, index):
        for shift in range(YS):
            for swapped in range(2):
                core = my_core if swapped == 0 else 1 - my_core
                origin = lax.rem(my_y - shift + YS, YS) * 2 + core
                at = pl.multiple_of(origin * PIECE, PIECE)
                tile[member, pl.ds(at, PIECE), :] = pieces[shift * 2 + swapped, index]
        return tile[member]

    return own, moved


def outer_kernel(place, own, sizes, moved, totals, near_hbm, stored_hbm, *refs):
    pieces_hbm, (out_hbm, near, stored, pieces, split, tile, sums, sems) = refs[:2 * YS], refs[2 * YS:]
    low_tile = place[0] * HERE
    sums[...] = jnp.zeros_like(sums)

    @pl.when(sizes[0] + totals[0] > 0)
    def _():
        copies = [
            pltpu.make_async_copy(near_hbm, near, sems.at[0]),
            pltpu.make_async_copy(stored_hbm, stored, sems.at[1]),
        ] + [pltpu.make_async_copy(pieces_hbm[k], pieces.at[k], sems.at[2 + k]) for k in range(2 * YS)]
        for copy in copies:
            copy.start()
        copies[0].wait()
        fill_split(split, near, 0)
        fetch_own, fetch_moved = fetchers(place, stored, pieces, tile)
        copies[1].wait()
        products_of(low_tile, own, 0, sizes[0], fetch_own, split, sums)
        for copy in copies[2:]:
            copy.wait()
        products_of(low_tile, moved, 0, totals[0], fetch_moved, split, sums)

    back = pltpu.make_async_copy(sums.at[pl.ds(ZS, 2)], out_hbm, sems.at[2 + 2 * YS])
    back.start()
    back.wait()


def inner_kernel(place, own, sizes, moved, totals, near_hbm, extra_hbm, stored_hbm, *refs):
    pieces_hbm, outs = refs[:2 * YS], refs[2 * YS:2 * YS + ZS + 1]
    near, extra, stored, pieces, split, tile, sums, sems = refs[2 * YS + ZS + 1:]
    low_tile = place[0] * HERE
    copies = [
        pltpu.make_async_copy(near_hbm, near, sems.at[0]),
        pltpu.make_async_copy(extra_hbm, extra, sems.at[1]),
        pltpu.make_async_copy(stored_hbm, stored, sems.at[2]),
    ] + [pltpu.make_async_copy(pieces_hbm[k], pieces.at[k], sems.at[3 + k]) for k in range(2 * YS)]
    for copy in copies:
        copy.start()
    sums[...] = jnp.zeros_like(sums)
    copies[0].wait()
    fill_split(split, near, 0)
    copies[1].wait()
    fill_split(split, extra, HERE)
    fetch_own, fetch_moved = fetchers(place, stored, pieces, tile)
    copies[2].wait()
    products_of(low_tile, own, XS * LIST, sizes[XS], fetch_own, split, sums)
    for copy in copies[3:]:
        copy.wait()
    products_of(low_tile, moved, LIST, totals[1], fetch_moved, split, sums)

    @pl.when(totals[2] > 0)
    def _():
        sums[...] = jnp.full_like(sums, jnp.nan)

    half = near.shape[1] // 2
    first_sem = 3 + 2 * YS
    backs = []
    for step in range(ZS + 1):
        block = lax.rem(place[2] + (step if step < ZS else ZS // 2), ZS)
        source = sums.at[block]
        if step == ZS // 2:
            source = sums.at[block, pl.ds(0, half)]
        if step == ZS:
            source = sums.at[block, pl.ds(half, half)]
        backs.append(pltpu.make_async_copy(source, outs[step], sems.at[first_sem + step]))
    for back in backs:
        back.start()
    for back in backs:
        back.wait()


def scratch_of(near, extra, integrals, sem_count):
    _, rows_here, wide = near.shape
    shapes = [near.shape] + ([extra.shape] if extra is not None else []) + [integrals.shape]
    return [pltpu.VMEM(shape, jnp.float32) for shape in shapes] + [
        pltpu.VMEM((2 * YS, TOTAL_CAP, PIECE, WIDTH), jnp.float32),
        pltpu.VMEM((HERE + EXTRA, rows_here, 2 * WIDTH), jnp.bfloat16),
        pltpu.VMEM((GROUP, WIDTH, WIDTH), jnp.float32),
        pltpu.VMEM((ZS + 3, rows_here, wide), jnp.float32),
        pltpu.SemaphoreType.DMA((sem_count,)),
    ]


def outer_sums(place, own, sizes, moved, totals, near, stored, pieces):
    _, rows_here, wide = near.shape
    smem = pl.BlockSpec(memory_space=pltpu.SMEM)
    anywhere = pl.BlockSpec(memory_space=pl.ANY)
    return pl.pallas_call(
        outer_kernel,
        in_specs=[smem] * 5 + [anywhere] * (2 + 2 * YS),
        out_specs=anywhere,
        out_shape=jax.ShapeDtypeStruct((2, rows_here, wide), jnp.float32),
        scratch_shapes=scratch_of(near, None, stored, 3 + 2 * YS),
        cost_estimate=pl.CostEstimate(flops=5 * 10**9, bytes_accessed=10**7, transcendentals=0),
        compiler_params=pltpu.CompilerParams(vmem_limit_bytes=28 * 2**20),
        name="outer",
    )(place, own, sizes, moved, totals, near, stored, *pieces)


def inner_sums(place, own, sizes, moved, totals, near, extra, stored, pieces):
    _, rows_here, wide = near.shape
    smem = pl.BlockSpec(memory_space=pltpu.SMEM)
    anywhere = pl.BlockSpec(memory_space=pl.ANY)
    heights = [rows_here] * (ZS // 2) + [rows_here // 2] + [rows_here] * (ZS // 2 - 1) + [rows_here // 2]
    return pl.pallas_call(
        inner_kernel,
        in_specs=[smem] * 5 + [anywhere] * (3 + 2 * YS),
        out_specs=[anywhere] * (ZS + 1),
        out_shape=[jax.ShapeDtypeStruct((height, wide), jnp.float32) for height in heights],
        scratch_shapes=scratch_of(near, extra, stored, 3 + 2 * YS + ZS + 1),
        cost_estimate=pl.CostEstimate(flops=10**10, bytes_accessed=10**7, transcendentals=0),
        compiler_params=pltpu.CompilerParams(vmem_limit_bytes=28 * 2**20),
        name="inner",
    )(place, own, sizes, moved, totals, near, extra, stored, *pieces)


def ring_sum(parts, more):
    half = ZS // 2
    rows_here = parts[0].shape[0]
    middle = more(half)
    up, down = parts[half] + middle[:rows_here // 2], parts[ZS] + middle[rows_here // 2:]
    for step in range(half - 1, -1, -1):
        up, down = lax.optimization_barrier((up, down))
        up = lax.ppermute(up, "tile", z_shift(1))
        down = lax.ppermute(down, "tile", z_shift(-1))
        up, down = lax.optimization_barrier((up, down))
        if step == half - 1:
            up = jnp.concatenate([up, jnp.zeros_like(up)], axis=0)
            down = jnp.concatenate([jnp.zeros_like(down), down], axis=0)
        if step > 0:
            up = up + parts[step] + more(step)
            down = down + parts[ZS - step] + more(ZS - step)
    return parts[0] + more(0) + up + down


def shards(
    amplitudes, driver, integrals, tile_rows, tile_cols, tile_count, pair_energy, virt_energy
):
    my_tile = lax.axis_index("tile")
    my_x = my_tile // ZS
    my_z = lax.rem(my_tile, ZS)
    place = jnp.stack([my_x, lax.axis_index("pair"), my_z]).astype(jnp.int32)

    near = lax.all_gather(amplitudes, "tile", axis=0, axis_index_groups=Z_GROUPS)

    *packed, own, sizes = pack(place, tile_rows, tile_cols, tile_count, integrals)
    arrived = [lax.ppermute(packed[step - 1], "tile", x_shift(step)) for step in range(1, XS)]
    mine, moved, totals = compact(place, sizes, arrived)
    along_y = [mine] + [lax.ppermute(mine, "pair", y_shift(step)) for step in range(1, YS)]
    along_y[1], near = lax.optimization_barrier((along_y[1], near))
    extra = lax.ppermute(near[:2], "tile", x_shift(-1))
    pieces = []
    for piece in along_y:
        pieces += [piece, lax.ppermute(piece, "pair", CORE_SWAP)]

    beyond = outer_sums(place, own, sizes, moved, totals, near, integrals, pieces)
    from_left = lax.ppermute(beyond, "tile", x_shift(1))
    parts = inner_sums(place, own, sizes, moved, totals, near, extra, integrals, pieces)

    def more(step):
        block = lax.rem(my_z + step, ZS)
        return jnp.where(
            (my_x > 0) & (block == 0), from_left[0], jnp.where((my_x > 0) & (block == 1), from_left[1], 0.0)
        )

    ladder = ring_sum(parts, more)
    denominator = virt_energy[None, :] - pair_energy[:, None]
    result = (driver + ladder) / denominator

    def slow():
        full = dense_ladder(amplitudes, integrals, tile_rows, tile_cols, tile_count)
        return (driver + full) / denominator

    return lax.cond(jnp.isnan(ladder[0, 0]), slow, lambda: result)


def solution(mesh):
    return jax.shard_map(
        shards,
        mesh=mesh,
        in_specs=(
            P("pair", "tile"),
            P("pair", "tile"),
            P("tile", None, None),
            P("tile"),
            P("tile"),
            P("tile"),
            P("pair"),
            P("tile"),
        ),
        out_specs=P("pair", "tile"),
        check_vma=False,
    )
```

```python
import jax
import jax.numpy as jnp
from jax import lax
from jax.experimental import pallas as pl
from jax.experimental.pallas import tpu as pltpu
from jax.sharding import PartitionSpec as P

XS = 4
ZS = 8
YS = 4
CAP = 32
TOTAL_CAP = 68
LIST = 72
GROUP = 4
EXTRA = 16
HERE = 64
PIECE = 16
WIDTH = 128

Z_GROUPS = [[x * ZS + z for z in range(ZS)] for x in range(XS)]


def x_shift(step):
    return [(x * ZS + z, ((x + step) % XS) * ZS + z) for x in range(XS) for z in range(ZS)]


def z_shift(step):
    return [(x * ZS + z, x * ZS + (z + step) % ZS) for x in range(XS) for z in range(ZS)]


def y_shift(step):
    return [(y * 2 + core, ((y + step) % YS) * 2 + core) for y in range(YS) for core in range(2)]


CORE_SWAP = [(y * 2 + core, y * 2 + 1 - core) for y in range(YS) for core in range(2)]


def contract(blocks, stored, row_list, col_list, live_count):
    tile_width = stored.shape[1]
    group_size = 8
    slot_total = stored.shape[0]
    rows_here = blocks.shape[0]
    groups = (live_count + group_size - 1) // group_size

    def group_step(group, totals):
        index_list = group * group_size + jnp.arange(group_size, dtype=jnp.int32)
        safe_index = jnp.minimum(index_list, slot_total - 1)
        pieces = jnp.take(stored, safe_index, axis=0)
        row_ids = jnp.take(row_list, safe_index, axis=0)
        col_ids = jnp.take(col_list, safe_index, axis=0)
        active = (index_list < live_count).astype(jnp.float32)
        inputs = jnp.take(blocks, row_ids, axis=1)
        product = jnp.einsum("pgk,gkn->pgn", inputs, pieces, precision=lax.Precision.HIGHEST)
        product = product * active[None, :, None]
        return totals.at[:, col_ids, :].add(product)

    start_totals = jnp.zeros((rows_here, blocks.shape[1], tile_width), jnp.float32)
    return lax.fori_loop(0, groups, group_step, start_totals)


def dense_ladder(amplitudes, integrals, tile_rows, tile_cols, tile_count):
    rows_here = amplitudes.shape[0]
    columns_all = amplitudes.shape[1] * lax.axis_size("tile")
    gathered = lax.all_gather(amplitudes, "tile", axis=1, tiled=True)
    blocks = gathered.reshape(rows_here, columns_all // WIDTH, WIDTH)
    partial_value = contract(blocks, integrals, tile_rows, tile_cols, tile_count[0])
    partial_value = partial_value.reshape(rows_here, columns_all)
    return lax.psum_scatter(partial_value, "tile", scatter_dimension=1, tiled=True)


def home(row, col):
    return jnp.minimum(row, col) // HERE


def pad_list(table, first, size, low):
    for pad in range(GROUP):
        table[0, first + size + pad] = 0
        table[1, first + size + pad] = low
        table[2, first + size + pad] = low + HERE + EXTRA


def pack_kernel(place, rows, cols, count, stored, *refs):
    outs, table, sizes, entries, sems = refs[:XS - 1], refs[XS - 1], refs[XS], refs[XS + 1], refs[XS + 2]
    mine = place[0]
    low = mine * HERE
    for each in range(8):
        sizes[each] = 0

    def sort_step(slot, _):
        row, col = rows[slot], cols[slot]
        target = lax.rem(home(row, col) - mine + XS, XS)
        kind = jnp.where(target == 0, jnp.where(col - low >= HERE, 0, XS), target)
        position = sizes[kind]
        at = kind * LIST + position
        table[0, at] = slot
        table[1, at] = row
        table[2, at] = col
        sizes[kind] = position + 1
        return 0

    lax.fori_loop(0, count[0], sort_step, 0)
    over = jnp.int32(0)
    for j in range(1, XS):
        over = jnp.maximum(over, (sizes[j] > CAP).astype(jnp.int32))
    sizes[XS + 1] = over
    pad_list(table, 0, sizes[0], low)
    pad_list(table, XS * LIST, sizes[XS], low)
    copies = []
    for j in range(1, XS):
        out = outs[j - 1]
        entries[j - 1, 2, 0] = over.astype(jnp.float32)
        entries[j - 1, 3, mine] = 0.0
        for other in range(1, XS):
            entries[j - 1, 3, lax.rem(mine + other, XS)] = sizes[other].astype(jnp.float32)

        def move_step(item, _):
            at = j * LIST + item
            out[item] = stored[table[0, at]]
            entries[j - 1, 0, item] = table[1, at].astype(jnp.float32)
            entries[j - 1, 1, item] = table[2, at].astype(jnp.float32)
            return 0

        lax.fori_loop(0, jnp.minimum(sizes[j], CAP), move_step, 0)
        copy = pltpu.make_async_copy(entries.at[j - 1], out.at[CAP, pl.ds(0, 8)], sems.at[j - 1])
        copy.start()
        copies.append(copy)
    for copy in copies:
        copy.wait()


def pack(place, rows, cols, count, integrals):
    slots = integrals.shape[0]
    spec = pltpu.PrefetchScalarGridSpec(
        num_scalar_prefetch=4,
        grid=(1,),
        in_specs=[pl.BlockSpec((slots, PIECE, WIDTH), lambda i, place, *_: (0, place[1], 0))],
        out_specs=[pl.BlockSpec((CAP + 1, PIECE, WIDTH), lambda i, *_: (0, 0, 0))] * (XS - 1)
        + [pl.BlockSpec(memory_space=pltpu.SMEM)] * 2,
        scratch_shapes=[pltpu.SMEM((XS - 1, 8, WIDTH), jnp.float32), pltpu.SemaphoreType.DMA((XS - 1,))],
    )
    return pl.pallas_call(
        pack_kernel,
        grid_spec=spec,
        out_shape=[jax.ShapeDtypeStruct((CAP + 1, PIECE, WIDTH), jnp.float32)] * (XS - 1)
        + [jax.ShapeDtypeStruct((3, (XS + 1) * LIST), jnp.int32), jax.ShapeDtypeStruct((8,), jnp.int32)],
        compiler_params=pltpu.CompilerParams(vmem_limit_bytes=8 * 2**20),
        name="pack",
    )(place, rows, cols, count, integrals)


def compact_kernel(place, sizes, *refs):
    sources, (out, table, totals, entries, sems) = refs[:XS - 1], refs[XS - 1:]
    mine = place[0]
    low = mine * HERE
    copies = [
        pltpu.make_async_copy(sources[j].at[CAP, pl.ds(0, 8)], entries.at[j], sems.at[j]) for j in range(XS - 1)
    ]
    for copy in copies:
        copy.start()
    for copy in copies:
        copy.wait()
    for each in range(8):
        totals[each] = 0
    over = sizes[XS + 1] > 0
    for j in range(XS - 1):
        over = over | (entries[j, 2, 0] > 0.5)
    for j in range(XS):
        there = lax.rem(mine + j, XS)
        total = jnp.int32(0) if j == 0 else sizes[j]
        for source in range(XS - 1):
            total = total + entries[source, 3, there].astype(jnp.int32)
        over = over | (total > TOTAL_CAP)
    for j in range(XS - 1):
        source = sources[j]
        size = jnp.minimum(entries[j, 3, mine].astype(jnp.int32), CAP)

        def step(item, _):
            row = entries[j, 0, item].astype(jnp.int32)
            col = entries[j, 1, item].astype(jnp.int32)
            far = col - low >= HERE
            kind = jnp.where(far, 0, 1)
            spot = jnp.minimum(totals[0] + totals[1], TOTAL_CAP - 1)
            out[spot] = source[item]
            position = jnp.minimum(totals[kind], TOTAL_CAP - 1)
            at = kind * LIST + position
            table[0, at] = spot
            table[1, at] = row
            table[2, at] = col
            totals[kind] = position + 1
            return 0

        lax.fori_loop(0, size, step, 0)
    totals[2] = over.astype(jnp.int32)
    pad_list(table, 0, totals[0], low)
    pad_list(table, LIST, totals[1], low)


def compact(place, sizes, sources):
    vmem = pl.BlockSpec(memory_space=pltpu.VMEM)
    smem = pl.BlockSpec(memory_space=pltpu.SMEM)
    return pl.pallas_call(
        compact_kernel,
        in_specs=[smem] * 2 + [vmem] * (XS - 1),
        out_specs=[vmem, smem, smem],
        out_shape=[
            jax.ShapeDtypeStruct((TOTAL_CAP, PIECE, WIDTH), jnp.float32),
            jax.ShapeDtypeStruct((3, 2 * LIST), jnp.int32),
            jax.ShapeDtypeStruct((8,), jnp.int32),
        ],
        scratch_shapes=[pltpu.SMEM((XS - 1, 8, WIDTH), jnp.float32), pltpu.SemaphoreType.DMA((XS - 1,))],
        compiler_params=pltpu.CompilerParams(vmem_limit_bytes=8 * 2**20),
        name="compact",
    )(place, sizes, *sources)


def split_of(value):
    high = value.astype(jnp.bfloat16)
    return high, (value - high.astype(jnp.float32)).astype(jnp.bfloat16)


def products_of(low_tile, table, first, size, load, left, tile, sums, first_block):
    blank = jnp.zeros((WIDTH, WIDTH), jnp.bfloat16)

    def step(group, _):
        start = first + group * GROUP
        load([table[0, start + member] for member in range(GROUP)])
        rows = [left(member, table[1, start + member] - low_tile) for member in range(GROUP)]
        products = []
        for member in range(GROUP):
            high, low = split_of(tile[member])
            right = jnp.concatenate(
                [jnp.concatenate([high, low], axis=1), jnp.concatenate([high, blank], axis=1)], axis=0
            )
            product = jnp.dot(rows[member], right, preferred_element_type=jnp.float32)
            products.append(product[:, :WIDTH] + product[:, WIDTH:])
        for member in range(GROUP):
            col = table[2, start + member] - low_tile
            lanes = pl.ds(pl.multiple_of(lax.rem(col, ZS) * WIDTH, WIDTH), WIDTH)
            sums[lax.div(col, ZS) - first_block, :, lanes] += products[member]
        return 0

    lax.fori_loop(0, lax.div(size + GROUP - 1, GROUP), step, 0)


def origins(place):
    my_y = lax.div(place[1], 2)
    my_core = lax.rem(place[1], 2)
    rows = []
    for shift in range(YS):
        for swapped in range(2):
            core = my_core if swapped == 0 else 1 - my_core
            rows.append(pl.multiple_of((lax.rem(my_y - shift + YS, YS) * 2 + core) * PIECE, PIECE))
    return rows


def load_own(stored_hbm, tile, sems):
    def load(indices):
        copies = [
            pltpu.make_async_copy(stored_hbm.at[indices[member]], tile.at[member], sems.at[member, 0])
            for member in range(GROUP)
        ]
        for copy in copies:
            copy.start()
        for copy in copies:
            copy.wait()

    return load


def outer_kernel(
    place, own, sizes, moved, totals, near_hbm, stored_hbm, *refs
):
    pieces_hbm, (out_hbm, block, tile, sums, sems, end) = refs[:2 * YS], refs[2 * YS:]
    low_tile = place[0] * HERE
    sums[...] = jnp.zeros_like(sums)
    rows_of = origins(place)

    def load_far(indices):
        copies = []
        for member in range(GROUP):
            for k in range(2 * YS):
                copies.append(
                    pltpu.make_async_copy(
                        pieces_hbm[k].at[indices[member]],
                        tile.at[member, pl.ds(rows_of[k], PIECE)],
                        sems.at[member, k],
                    )
                )
        for copy in copies:
            copy.start()
        for copy in copies:
            copy.wait()

    def left(member, row):
        lanes = pl.ds(pl.multiple_of(lax.rem(row, ZS) * WIDTH, WIDTH), WIDTH)
        copy = pltpu.make_async_copy(near_hbm.at[lax.div(row, ZS), :, lanes], block.at[member], sems.at[member, 2 * YS])
        copy.start()
        copy.wait()
        return jnp.concatenate(split_of(block[member]), axis=1)

    products_of(low_tile, own, 0, sizes[0], load_own(stored_hbm, tile, sems), left, tile, sums, ZS)
    products_of(low_tile, moved, 0, totals[0], load_far, left, tile, sums, ZS)
    back = pltpu.make_async_copy(sums.at[pl.ds(0, 2)], out_hbm, end.at[0])
    back.start()
    back.wait()


def inner_kernel(place, own, sizes, moved, totals, near_hbm, extra_hbm, stored_hbm, *refs):
    pieces_hbm, outs = refs[:2 * YS], refs[2 * YS:2 * YS + ZS + 1]
    near, extra, pieces, split, tile, sums, sems, tile_sems = refs[2 * YS + ZS + 1:]
    low_tile = place[0] * HERE
    copies = [
        pltpu.make_async_copy(near_hbm, near, sems.at[0]),
        pltpu.make_async_copy(extra_hbm, extra, sems.at[1]),
    ] + [pltpu.make_async_copy(pieces_hbm[k], pieces.at[k], sems.at[2 + k]) for k in range(2 * YS)]
    for copy in copies:
        copy.start()
    sums[...] = jnp.zeros_like(sums)
    copies[0].wait()
    for z in range(ZS):
        for part in range(ZS):
            high, low = split_of(near[z, :, part * WIDTH:(part + 1) * WIDTH])
            split[z * ZS + part, :, :WIDTH] = high
            split[z * ZS + part, :, WIDTH:] = low
    copies[1].wait()
    for z in range(2):
        for part in range(ZS):
            high, low = split_of(extra[z, :, part * WIDTH:(part + 1) * WIDTH])
            split[HERE + z * ZS + part, :, :WIDTH] = high
            split[HERE + z * ZS + part, :, WIDTH:] = low
    rows_of = origins(place)

    def load_moved(indices):
        for member in range(GROUP):
            for k in range(2 * YS):
                tile[member, pl.ds(rows_of[k], PIECE), :] = pieces[k, indices[member]]

    def left(member, row):
        return split[row]

    products_of(low_tile, own, XS * LIST, sizes[XS], load_own(stored_hbm, tile, tile_sems), left, tile, sums, 0)
    for copy in copies[2:]:
        copy.wait()
    products_of(low_tile, moved, LIST, totals[1], load_moved, left, tile, sums, 0)

    @pl.when(totals[2] > 0)
    def _():
        sums[...] = jnp.full_like(sums, jnp.nan)

    half = near.shape[1] // 2
    first_sem = 2 + 2 * YS
    backs = []
    for step in range(ZS + 1):
        block = lax.rem(place[2] + (step if step < ZS else ZS // 2), ZS)
        source = sums.at[block]
        if step == ZS // 2:
            source = sums.at[block, pl.ds(0, half)]
        if step == ZS:
            source = sums.at[block, pl.ds(half, half)]
        backs.append(pltpu.make_async_copy(source, outs[step], sems.at[first_sem + step]))
    for back in backs:
        back.start()
    for back in backs:
        back.wait()


def outer_sums(place, own, sizes, moved, totals, near, stored, pieces):
    _, rows_here, wide = near.shape
    smem = pl.BlockSpec(memory_space=pltpu.SMEM)
    hbm = pl.BlockSpec(memory_space=pltpu.HBM)
    return pl.pallas_call(
        outer_kernel,
        in_specs=[smem] * 5 + [hbm] * (2 + 2 * YS),
        out_specs=pl.BlockSpec(memory_space=pl.ANY),
        out_shape=jax.ShapeDtypeStruct((2, rows_here, wide), jnp.float32),
        scratch_shapes=[
            pltpu.VMEM((GROUP, rows_here, WIDTH), jnp.float32),
            pltpu.VMEM((GROUP, WIDTH, WIDTH), jnp.float32),
            pltpu.VMEM((3, rows_here, wide), jnp.float32),
            pltpu.SemaphoreType.DMA((GROUP, 2 * YS + 1)),
            pltpu.SemaphoreType.DMA((1,)),
        ],
        cost_estimate=pl.CostEstimate(flops=10**6, bytes_accessed=10**4, transcendentals=0),
        compiler_params=pltpu.CompilerParams(vmem_limit_bytes=4 * 2**20),
        name="outer",
    )(place, own, sizes, moved, totals, near, stored, *pieces)


def inner_sums(place, own, sizes, moved, totals, near, extra, stored, pieces):
    _, rows_here, wide = near.shape
    smem = pl.BlockSpec(memory_space=pltpu.SMEM)
    hbm = pl.BlockSpec(memory_space=pltpu.HBM)
    heights = [rows_here] * (ZS // 2) + [rows_here // 2] + [rows_here] * (ZS // 2 - 1) + [rows_here // 2]
    return pl.pallas_call(
        inner_kernel,
        in_specs=[smem] * 5 + [hbm] * (3 + 2 * YS),
        out_specs=[pl.BlockSpec(memory_space=pl.ANY)] * (ZS + 1),
        out_shape=[jax.ShapeDtypeStruct((height, wide), jnp.float32) for height in heights],
        scratch_shapes=[
            pltpu.VMEM(near.shape, jnp.float32),
            pltpu.VMEM(extra.shape, jnp.float32),
            pltpu.VMEM((2 * YS, TOTAL_CAP, PIECE, WIDTH), jnp.float32),
            pltpu.VMEM((HERE + EXTRA, rows_here, 2 * WIDTH), jnp.bfloat16),
            pltpu.VMEM((GROUP, WIDTH, WIDTH), jnp.float32),
            pltpu.VMEM((ZS + 3, rows_here, wide), jnp.float32),
            pltpu.SemaphoreType.DMA((2 + 2 * YS + ZS + 1,)),
            pltpu.SemaphoreType.DMA((GROUP, 1)),
        ],
        cost_estimate=pl.CostEstimate(flops=10**10, bytes_accessed=10**7, transcendentals=0),
        compiler_params=pltpu.CompilerParams(vmem_limit_bytes=18 * 2**20),
        name="inner",
    )(place, own, sizes, moved, totals, near, extra, stored, *pieces)


def ring_sum(parts, more):
    half = ZS // 2
    rows_here = parts[0].shape[0]
    middle = more(half)
    up, down = parts[half] + middle[:rows_here // 2], parts[ZS] + middle[rows_here // 2:]
    for step in range(half - 1, -1, -1):
        up, down = lax.optimization_barrier((up, down))
        up = lax.ppermute(up, "tile", z_shift(1))
        down = lax.ppermute(down, "tile", z_shift(-1))
        up, down = lax.optimization_barrier((up, down))
        if step == half - 1:
            up = jnp.concatenate([up, jnp.zeros_like(up)], axis=0)
            down = jnp.concatenate([jnp.zeros_like(down), down], axis=0)
        if step > 0:
            up = up + parts[step] + more(step)
            down = down + parts[ZS - step] + more(ZS - step)
    return parts[0] + more(0) + up + down


def shards(
    amplitudes, driver, integrals, tile_rows, tile_cols, tile_count, pair_energy, virt_energy
):
    my_tile = lax.axis_index("tile")
    my_x = my_tile // ZS
    my_z = lax.rem(my_tile, ZS)
    place = jnp.stack([my_x, lax.axis_index("pair"), my_z]).astype(jnp.int32)

    near = lax.all_gather(amplitudes, "tile", axis=0, axis_index_groups=Z_GROUPS)

    *packed, own, sizes = pack(place, tile_rows, tile_cols, tile_count, integrals)
    arrived = [lax.ppermute(packed[step - 1], "tile", x_shift(step)) for step in range(1, XS)]
    mine, moved, totals = compact(place, sizes, arrived)
    along_y = [mine] + [lax.ppermute(mine, "pair", y_shift(step)) for step in range(1, YS)]
    across = lax.ppermute(mine, "pair", CORE_SWAP)
    along_y[YS - 1], across = lax.optimization_barrier((along_y[YS - 1], across))
    first = near[:2]
    extra = lax.ppermute(first, "tile", x_shift(-1))
    along_y[1], along_y[2], first = lax.optimization_barrier((along_y[1], along_y[2], first))
    pieces = [mine, across]
    for piece in along_y[1:]:
        pieces += [piece, lax.ppermute(piece, "pair", CORE_SWAP)]
    beyond = outer_sums(place, own, sizes, moved, totals, near, integrals, pieces)
    from_left = lax.ppermute(beyond, "tile", x_shift(1))
    parts = inner_sums(place, own, sizes, moved, totals, near, extra, integrals, pieces)

    def more(step):
        block = lax.rem(my_z + step, ZS)
        return jnp.where(block == 0, from_left[0], jnp.where(block == 1, from_left[1], 0.0))

    ladder = ring_sum(parts, more)
    denominator = virt_energy[None, :] - pair_energy[:, None]
    result = (driver + ladder) / denominator

    def slow():
        full = dense_ladder(amplitudes, integrals, tile_rows, tile_cols, tile_count)
        return (driver + full) / denominator

    return lax.cond(jnp.isnan(ladder[0, 0]), slow, lambda: result)


def solution(mesh):
    return jax.shard_map(
        shards,
        mesh=mesh,
        in_specs=(
            P("pair", "tile"),
            P("pair", "tile"),
            P("tile", None, None),
            P("tile"),
            P("tile"),
            P("tile"),
            P("pair"),
            P("tile"),
        ),
        out_specs=P("pair", "tile"),
        check_vma=False,
    )
```

```python
import jax
import jax.numpy as jnp
from jax import lax
from jax.experimental import pallas as pl
from jax.experimental.pallas import tpu as pltpu
from jax.sharding import PartitionSpec as P

XS = 4
ZS = 8
YS = 4
CAP = 32
TOTAL_CAP = 68
LIST = 72
GROUP = 4
EXTRA = 16
ROUND = 16
LIMIT = 56
HERE = 64
PIECE = 16
WIDTH = 128

Z_GROUPS = [[x * ZS + z for z in range(ZS)] for x in range(XS)]


def x_shift(step):
    return [(x * ZS + z, ((x + step) % XS) * ZS + z) for x in range(XS) for z in range(ZS)]


def z_shift(step):
    return [(x * ZS + z, x * ZS + (z + step) % ZS) for x in range(XS) for z in range(ZS)]


def y_shift(step):
    return [(y * 2 + core, ((y + step) % YS) * 2 + core) for y in range(YS) for core in range(2)]


CORE_SWAP = [(y * 2 + core, y * 2 + 1 - core) for y in range(YS) for core in range(2)]


def contract(blocks, stored, row_list, col_list, live_count):
    tile_width = stored.shape[1]
    group_size = 8
    slot_total = stored.shape[0]
    rows_here = blocks.shape[0]
    groups = (live_count + group_size - 1) // group_size

    def group_step(group, totals):
        index_list = group * group_size + jnp.arange(group_size, dtype=jnp.int32)
        safe_index = jnp.minimum(index_list, slot_total - 1)
        pieces = jnp.take(stored, safe_index, axis=0)
        row_ids = jnp.take(row_list, safe_index, axis=0)
        col_ids = jnp.take(col_list, safe_index, axis=0)
        active = (index_list < live_count).astype(jnp.float32)
        inputs = jnp.take(blocks, row_ids, axis=1)
        product = jnp.einsum("pgk,gkn->pgn", inputs, pieces, precision=lax.Precision.HIGHEST)
        product = product * active[None, :, None]
        return totals.at[:, col_ids, :].add(product)

    start_totals = jnp.zeros((rows_here, blocks.shape[1], tile_width), jnp.float32)
    return lax.fori_loop(0, groups, group_step, start_totals)


def dense_ladder(amplitudes, integrals, tile_rows, tile_cols, tile_count):
    rows_here = amplitudes.shape[0]
    columns_all = amplitudes.shape[1] * lax.axis_size("tile")
    gathered = lax.all_gather(amplitudes, "tile", axis=1, tiled=True)
    blocks = gathered.reshape(rows_here, columns_all // WIDTH, WIDTH)
    partial_value = contract(blocks, integrals, tile_rows, tile_cols, tile_count[0])
    partial_value = partial_value.reshape(rows_here, columns_all)
    return lax.psum_scatter(partial_value, "tile", scatter_dimension=1, tiled=True)


def home(row, col):
    return jnp.minimum(row, col) // HERE


class Part:
    def __init__(self, ref, first, width=0):
        self.ref, self.first, self.width = ref, first, width

    def spot(self, key):
        if isinstance(key, tuple):
            return self.first + key[0] * self.width + key[1]
        return self.first + key

    def __getitem__(self, key):
        return self.ref[self.spot(key)]

    def __setitem__(self, key, value):
        self.ref[self.spot(key)] = value


OWN_WIDTH = (XS + 1) * LIST
MOVED_WIDTH = 2 * LIST


def own_parts(ref):
    return Part(ref, 0), Part(ref, 8), Part(ref, 16, OWN_WIDTH)


def moved_parts(ref):
    return Part(ref, 0), Part(ref, 8, MOVED_WIDTH)


def pad_list(table, first, size, row, col):
    for pad in range(GROUP):
        table[0, first + size + pad] = 0
        table[1, first + size + pad] = row
        table[2, first + size + pad] = col


def pack_kernel(facts, stored, *refs):
    outs, (plan, mine_of, entries, sems) = refs[:XS - 1], refs[XS - 1:]
    slots = stored.shape[0]
    rows, cols = Part(facts, 8), Part(facts, 8 + slots)
    place, sizes, table = own_parts(plan)
    for each in range(3):
        place[each] = facts[each]
    mine = place[0]
    low = mine * HERE
    fetch = pltpu.make_async_copy(stored.at[:, pl.ds(pl.multiple_of(place[1] * PIECE, PIECE), PIECE)], mine_of, sems.at[XS - 1])
    fetch.start()
    for each in range(8):
        sizes[each] = 0

    def sort_step(slot, _):
        row, col = rows[slot], cols[slot]
        target = lax.rem(home(row, col) - mine + XS, XS)
        kind = jnp.where((target == 0) & (row - low >= HERE), XS, target)
        position = sizes[kind]
        at = kind * LIST + position
        table[0, at] = slot
        table[1, at] = row
        table[2, at] = col
        sizes[kind] = position + 1
        return 0

    lax.fori_loop(0, facts[3], sort_step, 0)
    over = jnp.int32(0)
    for j in range(1, XS):
        over = jnp.maximum(over, (sizes[j] > CAP).astype(jnp.int32))
    sizes[XS + 1] = over
    fetch.wait()
    pad_list(table, 0, sizes[0], low, low + HERE + EXTRA)
    pad_list(table, XS * LIST, sizes[XS], low + HERE, low + HERE)
    copies = []
    for j in range(1, XS):
        out = outs[j - 1]
        entries[j - 1, 2, 0] = over.astype(jnp.float32)
        entries[j - 1, 3, mine] = 0.0
        for other in range(1, XS):
            entries[j - 1, 3, lax.rem(mine + other, XS)] = sizes[other].astype(jnp.float32)

        def move_step(item, _):
            at = j * LIST + item
            out[item] = mine_of[table[0, at]]
            entries[j - 1, 0, item] = table[1, at].astype(jnp.float32)
            entries[j - 1, 1, item] = table[2, at].astype(jnp.float32)
            return 0

        lax.fori_loop(0, jnp.minimum(sizes[j], CAP), move_step, 0)
        copy = pltpu.make_async_copy(entries.at[j - 1], out.at[CAP, pl.ds(0, 8)], sems.at[j - 1])
        copy.start()
        copies.append(copy)
    for copy in copies:
        copy.wait()


def pack(facts, integrals):
    slots = integrals.shape[0]
    spec = pltpu.PrefetchScalarGridSpec(
        num_scalar_prefetch=1,
        grid=(1,),
        in_specs=[pl.BlockSpec(memory_space=pl.ANY)],
        out_specs=[pl.BlockSpec((CAP + 1, PIECE, WIDTH), lambda i, *_: (0, 0, 0))] * (XS - 1)
        + [pl.BlockSpec(memory_space=pltpu.SMEM)],
        scratch_shapes=[
            pltpu.VMEM((slots, PIECE, WIDTH), jnp.float32),
            pltpu.SMEM((XS - 1, 8, WIDTH), jnp.float32),
            pltpu.SemaphoreType.DMA((XS,)),
        ],
    )
    return pl.pallas_call(
        pack_kernel,
        grid_spec=spec,
        out_shape=[jax.ShapeDtypeStruct((CAP + 1, PIECE, WIDTH), jnp.float32)] * (XS - 1)
        + [jax.ShapeDtypeStruct((16 + 3 * OWN_WIDTH,), jnp.int32)],
        compiler_params=pltpu.CompilerParams(vmem_limit_bytes=8 * 2**20),
        name="pack",
    )(facts, integrals)


def compact_kernel(plan, *refs):
    sources, (out, moved_plan, entries, sems) = refs[:XS - 1], refs[XS - 1:]
    place, sizes, _ = own_parts(plan)
    totals, table = moved_parts(moved_plan)
    mine = place[0]
    low = mine * HERE
    copies = [
        pltpu.make_async_copy(sources[j].at[CAP, pl.ds(0, 8)], entries.at[j], sems.at[j]) for j in range(XS - 1)
    ]
    for copy in copies:
        copy.start()
    for copy in copies:
        copy.wait()
    for each in range(8):
        totals[each] = 0
    over = sizes[XS + 1] > 0
    for j in range(XS - 1):
        over = over | (entries[j, 2, 0] > 0.5)
    for j in range(XS):
        there = lax.rem(mine + j, XS)
        total = jnp.int32(0) if j == 0 else sizes[j]
        for source in range(XS - 1):
            total = total + entries[source, 3, there].astype(jnp.int32)
        over = over | (total > TOTAL_CAP)
    for j in range(XS - 1):
        source = sources[j]
        size = jnp.minimum(entries[j, 3, mine].astype(jnp.int32), CAP)

        def step(item, _):
            row = entries[j, 0, item].astype(jnp.int32)
            col = entries[j, 1, item].astype(jnp.int32)
            kind = jnp.where(row - low >= HERE, 1, 0)
            position = jnp.minimum(totals[kind], TOTAL_CAP - 1)
            out[jnp.where(kind == 1, TOTAL_CAP - 1 - position, position)] = source[item]
            at = kind * LIST + position
            table[1, at] = row
            table[2, at] = col
            totals[kind] = position + 1
            return 0

        lax.fori_loop(0, size, step, 0)
    totals[2] = over.astype(jnp.int32)
    pad_list(table, 0, totals[0], low, low + HERE + EXTRA)
    pad_list(table, LIST, totals[1], low + HERE, low + HERE)


def compact(plan, sources):
    vmem = pl.BlockSpec(memory_space=pltpu.VMEM)
    smem = pl.BlockSpec(memory_space=pltpu.SMEM)
    return pl.pallas_call(
        compact_kernel,
        in_specs=[smem] + [vmem] * (XS - 1),
        out_specs=[vmem, smem],
        out_shape=[
            jax.ShapeDtypeStruct((TOTAL_CAP, PIECE, WIDTH), jnp.float32),
            jax.ShapeDtypeStruct((8 + 3 * MOVED_WIDTH,), jnp.int32),
        ],
        scratch_shapes=[pltpu.SMEM((XS - 1, 8, WIDTH), jnp.float32), pltpu.SemaphoreType.DMA((XS - 1,))],
        compiler_params=pltpu.CompilerParams(vmem_limit_bytes=8 * 2**20),
        name="compact",
    )(plan, *sources)


def split_of(value):
    high = value.astype(jnp.bfloat16)
    return high, (value - high.astype(jnp.float32)).astype(jnp.bfloat16)


def products_of(low, table, first, size, left, fetch, sums):
    blank = jnp.zeros((WIDTH, WIDTH), jnp.bfloat16)

    def step(group, _):
        products = []
        for member in range(GROUP):
            item = group * GROUP + member
            high, rest = split_of(fetch(member, item, table[0, first + item]))
            right = jnp.concatenate(
                [jnp.concatenate([high, rest], axis=1), jnp.concatenate([high, blank], axis=1)], axis=0
            )
            product = jnp.dot(left(table[1, first + item] - low), right, preferred_element_type=jnp.float32)
            products.append(product[:, :WIDTH] + product[:, WIDTH:])
        for member in range(GROUP):
            col = table[2, first + group * GROUP + member] - low
            lanes = pl.ds(pl.multiple_of(lax.rem(col, ZS) * WIDTH, WIDTH), WIDTH)
            sums[lax.div(col, ZS), :, lanes] += products[member]
        return 0

    lax.fori_loop(0, lax.div(size + GROUP - 1, GROUP), step, 0)


def split_at(source, row):
    lanes = pl.ds(pl.multiple_of(lax.rem(row, ZS) * WIDTH, WIDTH), WIDTH)
    return jnp.concatenate(split_of(source[lax.div(row, ZS), :, lanes]), axis=1)


def start_own(table, first, size, stored_hbm, stored, sems):
    def step(item, _):
        pltpu.make_async_copy(stored_hbm.at[table[0, first + item]], stored.at[item], sems.at[item]).start()
        return 0

    lax.fori_loop(0, size, step, 0)


def wait_own(size, stored_hbm, stored, sems):
    def step(item, _):
        pltpu.make_async_copy(stored_hbm.at[0], stored.at[item], sems.at[item]).wait()
        return 0

    lax.fori_loop(0, size, step, 0)


def piece_rows(place):
    my_y = lax.div(place[1], 2)
    my_core = lax.rem(place[1], 2)
    rows = []
    for shift in range(YS):
        for swapped in range(2):
            core = my_core if swapped == 0 else 1 - my_core
            rows.append(pl.multiple_of((lax.rem(my_y - shift + YS, YS) * 2 + core) * PIECE, PIECE))
    return rows


def prepare_kernel(near_hbm, split_hbm, first_hbm, near, split, sems):
    copies = [pltpu.make_async_copy(near_hbm.at[z], near.at[z], sems.at[z]) for z in range(ZS)]
    for copy in copies:
        copy.start()
    backs = []
    for z in range(ZS):
        copies[z].wait()
        if z == 1:
            firsts = pltpu.make_async_copy(near.at[pl.ds(0, 2)], first_hbm, sems.at[ZS])
            firsts.start()
        for part in range(ZS):
            value = near[z, :, part * WIDTH:(part + 1) * WIDTH]
            split[z * ZS + part] = jnp.concatenate(split_of(value), axis=1)
        back = pltpu.make_async_copy(split.at[pl.ds(z * ZS, ZS)], split_hbm.at[pl.ds(z * ZS, ZS)], sems.at[ZS + 1 + z])
        back.start()
        backs.append(back)
    firsts.wait()
    for back in backs:
        back.wait()


def prepare(near):
    _, rows_here, wide = near.shape
    return pl.pallas_call(
        prepare_kernel,
        in_specs=[pl.BlockSpec(memory_space=pl.ANY)],
        out_specs=[pl.BlockSpec(memory_space=pl.ANY)] * 2,
        out_shape=[
            jax.ShapeDtypeStruct((HERE, rows_here, 2 * WIDTH), jnp.bfloat16),
            jax.ShapeDtypeStruct((2, rows_here, wide), jnp.float32),
        ],
        scratch_shapes=[
            pltpu.VMEM(near.shape, jnp.float32),
            pltpu.VMEM((HERE, rows_here, 2 * WIDTH), jnp.bfloat16),
            pltpu.SemaphoreType.DMA((2 * ZS + 1,)),
        ],
        compiler_params=pltpu.CompilerParams(vmem_limit_bytes=LIMIT * 2**20),
        name="prepare",
    )(near)


def chunk_copies(pieces_hbm, tiles, sems, rows_of, source, target, size):
    return [
        pltpu.make_async_copy(
            pieces_hbm[k].at[pl.ds(source, size)],
            tiles.at[pl.ds(target, size), pl.ds(rows_of[k], PIECE)],
            sems.at[target // ROUND, k],
        )
        for k in range(2 * YS)
    ]


def main_kernel(plan, moved_plan, split_hbm, stored_hbm, *refs):
    place, sizes, own = own_parts(plan)
    totals, moved = moved_parts(moved_plan)
    pieces_hbm, refs = refs[:2 * YS], refs[2 * YS:]
    out_hbm, soon_hbm, later_hbm, stored, tiles, sums, split, sems, own_sems, tile_sems = refs
    low = place[0] * HERE
    rows_of = piece_rows(place)
    copies = [
        pltpu.make_async_copy(split_hbm.at[pl.ds(z * ZS, ZS)], split.at[pl.ds(z * ZS, ZS)], sems.at[z])
        for z in range(ZS)
    ]
    for copy in copies:
        copy.start()
    start_own(own, 0, sizes[0], stored_hbm, stored, own_sems)
    chunks = []
    for first in range(0, TOTAL_CAP - ROUND + 1, ROUND):
        size = ROUND if first + 2 * ROUND <= TOTAL_CAP else TOTAL_CAP - first
        chunks.append((first, size, chunk_copies(pieces_hbm, tiles, tile_sems, rows_of, first, first, size)))
    for first, size, chunk in chunks:
        for copy in chunk:
            pl.when(totals[0] > first)(copy.start)
    sums[...] = jnp.zeros_like(sums)
    left = lambda row: split[row]
    for copy in copies:
        copy.wait()
    wait_own(sizes[0], stored_hbm, stored, own_sems)
    products_of(low, own, 0, sizes[0], left, lambda member, item, index: stored[item], sums)
    for first, size, chunk in chunks:
        for copy in chunk:
            pl.when(totals[0] > first)(copy.wait)
        here = jnp.clip(totals[0] - first, 0, size)
        products_of(low, moved, first, here, left, lambda member, item, index, first=first: tiles[first + item], sums)
    soon = jnp.where(place[2] == ZS // 2 + 1, 1, 0)
    last = ZS
    backs = [
        pltpu.make_async_copy(sums.at[ZS + soon], soon_hbm, sems.at[last]),
        pltpu.make_async_copy(sums.at[ZS + 1 - soon], later_hbm, sems.at[last + 1]),
    ]
    for z in range(ZS):
        block = lax.rem(place[2] + z, ZS)
        backs.append(pltpu.make_async_copy(sums.at[block], out_hbm.at[z], sems.at[last + 2 + z]))
    for back in backs:
        back.start()
    for back in backs:
        back.wait()


def late_kernel(plan, moved_plan, sums_in, extra_hbm, stored_hbm, *refs):
    place, sizes, own = own_parts(plan)
    totals, moved = moved_parts(moved_plan)
    pieces_hbm, refs = refs[:2 * YS], refs[2 * YS:]
    sums_hbm, extra, own_tiles, moved_tiles, sums, touched, sems, own_sems, moved_sems = refs
    low = place[0] * HERE
    rows_of = piece_rows(place)
    over = totals[2]
    own_first = XS * LIST

    left = lambda row: split_at(extra, row - HERE)

    def start_round(turn):
        start_own(own, own_first + turn * ROUND, own_here(turn), stored_hbm, own_tiles, own_sems)
        base = jnp.maximum(TOTAL_CAP - ROUND * (turn + 1), 0)
        chunk = chunk_copies(pieces_hbm, moved_tiles, moved_sems, rows_of, base, 0, ROUND)
        for copy in chunk:
            pl.when(moved_here(turn) > 0)(copy.start)
        return base, chunk

    def finish_round(turn, base, chunk):
        wait_own(own_here(turn), stored_hbm, own_tiles, own_sems)
        products_of(
            low, own, own_first + turn * ROUND, own_here(turn), left, lambda member, item, index: own_tiles[item], sums
        )
        for copy in chunk:
            pl.when(moved_here(turn) > 0)(copy.wait)

        def fetch(member, item, index):
            return moved_tiles[jnp.maximum(TOTAL_CAP - 1 - turn * ROUND - item - base, 0)]

        products_of(low, moved, LIST + turn * ROUND, moved_here(turn), left, fetch, sums)

    def own_here(turn):
        return jnp.clip(sizes[XS] - turn * ROUND, 0, ROUND)

    def moved_here(turn):
        return jnp.clip(totals[1] - turn * ROUND, 0, ROUND)

    def whole_round(turn, _):
        finish_round(turn, *start_round(turn))
        return 0

    def touch(table, first, size):
        def one(item, _):
            touched[lax.div(table[2, first + item] - low, ZS)] = 1
            return 0

        lax.fori_loop(0, size, one, 0)

    def spot(z):
        return lax.rem(z - place[2] + ZS, ZS)


    @pl.when((sizes[XS] + totals[1] > 0) & (over == 0))
    def _():
        first_round = start_round(0)
        copies = [pltpu.make_async_copy(extra_hbm.at[z], extra.at[z], sems.at[ZS + z]) for z in range(2)]
        for copy in copies:
            copy.start()
        for z in range(ZS):
            touched[z] = 0
        touch(own, own_first, sizes[XS])
        touch(moved, LIST, totals[1])
        inward = [pltpu.make_async_copy(sums_in.at[spot(z)], sums.at[z], sems.at[z]) for z in range(ZS)]
        outward = [pltpu.make_async_copy(sums.at[z], sums_hbm.at[spot(z)], sems.at[z]) for z in range(ZS)]
        for z in range(ZS):
            pl.when(touched[z] > 0)(inward[z].start)
        sums[ZS] = jnp.zeros(sums.shape[1:], jnp.float32)
        for copy in copies:
            copy.wait()
        for z in range(ZS):
            pl.when(touched[z] > 0)(inward[z].wait)
        finish_round(0, *first_round)
        rounds = lax.div(jnp.maximum(sizes[XS], totals[1]) + ROUND - 1, ROUND)
        lax.fori_loop(1, rounds, whole_round, 0)
        for z in range(ZS):
            pl.when(touched[z] > 0)(outward[z].start)
        for z in range(ZS):
            pl.when(touched[z] > 0)(outward[z].wait)

    @pl.when(over > 0)
    def _():
        sums[...] = jnp.full_like(sums, jnp.nan)
        whole = pltpu.make_async_copy(sums.at[pl.ds(0, ZS)], sums_hbm, sems.at[0])
        whole.start()
        whole.wait()


def call(kernel, name, scalars, arrays, outs, scratch, aliases):
    smem = pl.BlockSpec(memory_space=pltpu.SMEM)
    anywhere = pl.BlockSpec(memory_space=pl.ANY)
    return pl.pallas_call(
        kernel,
        in_specs=[smem] * len(scalars) + [anywhere] * len(arrays),
        out_specs=[anywhere] * len(outs),
        out_shape=[jax.ShapeDtypeStruct(shape, jnp.float32) for shape in outs],
        input_output_aliases=aliases,
        scratch_shapes=scratch,
        cost_estimate=pl.CostEstimate(flops=10**6, bytes_accessed=10**4, transcendentals=0),
        compiler_params=pltpu.CompilerParams(vmem_limit_bytes=LIMIT * 2**20),
        name=name,
    )(*scalars, *arrays)


def main_sums(scalars, split, stored, pieces, wide):
    rows_here = split.shape[1]
    scratch = [
        pltpu.VMEM((LIST,) + stored.shape[1:], jnp.float32),
        pltpu.VMEM((TOTAL_CAP + GROUP, WIDTH, WIDTH), jnp.float32),
        pltpu.VMEM((ZS + 3, rows_here, wide), jnp.float32),
        pltpu.VMEM(split.shape, jnp.bfloat16),
        pltpu.SemaphoreType.DMA((2 * ZS + 2,)),
        pltpu.SemaphoreType.DMA((LIST,)),
        pltpu.SemaphoreType.DMA((TOTAL_CAP // ROUND + 1, 2 * YS)),
    ]
    outs = [(ZS, rows_here, wide)] + [(rows_here, wide)] * 2
    return call(main_kernel, "main", scalars, [split, stored, *pieces], outs, scratch, {})


def late_sums(scalars, sums, extra, stored, pieces):
    _, rows_here, wide = sums.shape
    scratch = [
        pltpu.VMEM(extra.shape, jnp.float32),
        pltpu.VMEM((ROUND + GROUP, WIDTH, WIDTH), jnp.float32),
        pltpu.VMEM((ROUND, WIDTH, WIDTH), jnp.float32),
        pltpu.VMEM((ZS + 1, rows_here, wide), jnp.float32),
        pltpu.SMEM((ZS,), jnp.int32),
        pltpu.SemaphoreType.DMA((ZS + 2,)),
        pltpu.SemaphoreType.DMA((ROUND,)),
        pltpu.SemaphoreType.DMA((1, 2 * YS)),
    ]
    return call(late_kernel, "late", scalars, [sums, extra, stored, *pieces], [sums.shape], scratch, {2: 0})[0]


def ring_sum(sums, more):
    half = ZS // 2
    middle = sums[half] + more(half)
    rows_here = middle.shape[0]
    up, down = middle[:rows_here // 2], middle[rows_here // 2:]
    for step in range(half - 1, -1, -1):
        up, down = lax.optimization_barrier((up, down))
        up = lax.ppermute(up, "tile", z_shift(1))
        down = lax.ppermute(down, "tile", z_shift(-1))
        up, down = lax.optimization_barrier((up, down))
        if step == half - 1:
            up = jnp.concatenate([up, jnp.zeros_like(up)], axis=0)
            down = jnp.concatenate([jnp.zeros_like(down), down], axis=0)
        if step > 0:
            up = up + (sums[step] + more(step))
            down = down + (sums[ZS - step] + more(ZS - step))
    return sums[0] + more(0) + up + down


def shards(
    amplitudes, driver, integrals, tile_rows, tile_cols, tile_count, pair_energy, virt_energy
):
    my_tile = lax.axis_index("tile")
    my_x = my_tile // ZS
    my_z = lax.rem(my_tile, ZS)
    place = jnp.stack([my_x, lax.axis_index("pair"), my_z, tile_count[0], my_x, my_x, my_x, my_x]).astype(jnp.int32)
    facts = jnp.concatenate([place, tile_rows, tile_cols])

    near = lax.all_gather(amplitudes, "tile", axis=0, axis_index_groups=Z_GROUPS)

    *packed, plan = pack(facts, integrals)
    arrived = [lax.ppermute(packed[step - 1], "tile", x_shift(step)) for step in range(1, XS)]
    mine, moved_plan = compact(plan, arrived)
    along_y = [mine] + [lax.ppermute(mine, "pair", y_shift(step)) for step in range(1, YS)]
    across = lax.ppermute(mine, "pair", CORE_SWAP)
    along_y[YS - 1], across = lax.optimization_barrier((along_y[YS - 1], across))
    split, first = prepare(near)
    extra = lax.ppermute(first, "tile", x_shift(-1))
    along_y[1], along_y[2], first = lax.optimization_barrier((along_y[1], along_y[2], first))
    pieces = [mine, across]
    for piece in along_y[1:]:
        pieces += [piece, lax.ppermute(piece, "pair", CORE_SWAP)]
    scalars = (plan, moved_plan)
    sums, soon, later = main_sums(scalars, split, integrals, pieces, near.shape[2])
    soon = lax.ppermute(soon, "tile", x_shift(1))
    later = lax.ppermute(later, "tile", x_shift(1))
    sums = late_sums(scalars, sums, extra, integrals, pieces)
    soon_block = jnp.where(my_z == ZS // 2 + 1, 1, 0)

    def more(step):
        block = lax.rem(my_z + step, ZS)
        value = jnp.where(block == soon_block, soon, 0.0)
        if step == ZS // 2:
            return value
        return jnp.where(block == 1 - soon_block, later, value)

    ladder = ring_sum(sums, more)
    denominator = virt_energy[None, :] - pair_energy[:, None]
    result = (driver + ladder) / denominator

    def slow():
        full = dense_ladder(amplitudes, integrals, tile_rows, tile_cols, tile_count)
        return (driver + full) / denominator

    return lax.cond(jnp.isnan(ladder[0, 0]), slow, lambda: result)


def solution(mesh):
    return jax.shard_map(
        shards,
        mesh=mesh,
        in_specs=(
            P("pair", "tile"),
            P("pair", "tile"),
            P("tile", None, None),
            P("tile"),
            P("tile"),
            P("tile"),
            P("pair"),
            P("tile"),
        ),
        out_specs=P("pair", "tile"),
        check_vma=False,
    )
```

```python
import jax
import jax.numpy as jnp
from jax import lax
from jax.experimental import pallas as pl
from jax.experimental.pallas import tpu as pltpu
from jax.sharding import PartitionSpec as P

XS = 4
ZS = 8
YS = 4
CAP = 32
TOTAL_CAP = 68
LIST = 72
GROUP = 8
EXTRA = 16
ROUND = 16
LIMIT = 53
HERE = 64
PIECE = 16
WIDTH = 128

Z_GROUPS = [[x * ZS + z for z in range(ZS)] for x in range(XS)]


def x_shift(step):
    return [(x * ZS + z, ((x + step) % XS) * ZS + z) for x in range(XS) for z in range(ZS)]


def z_shift(step):
    return [(x * ZS + z, x * ZS + (z + step) % ZS) for x in range(XS) for z in range(ZS)]


def y_shift(step):
    return [(y * 2 + core, ((y + step) % YS) * 2 + core) for y in range(YS) for core in range(2)]


CORE_SWAP = [(y * 2 + core, y * 2 + 1 - core) for y in range(YS) for core in range(2)]


def contract(blocks, stored, row_list, col_list, live_count):
    tile_width = stored.shape[1]
    group_size = 8
    slot_total = stored.shape[0]
    rows_here = blocks.shape[0]
    groups = (live_count + group_size - 1) // group_size

    def group_step(group, totals):
        index_list = group * group_size + jnp.arange(group_size, dtype=jnp.int32)
        safe_index = jnp.minimum(index_list, slot_total - 1)
        pieces = jnp.take(stored, safe_index, axis=0)
        row_ids = jnp.take(row_list, safe_index, axis=0)
        col_ids = jnp.take(col_list, safe_index, axis=0)
        active = (index_list < live_count).astype(jnp.float32)
        inputs = jnp.take(blocks, row_ids, axis=1)
        product = jnp.einsum("pgk,gkn->pgn", inputs, pieces, precision=lax.Precision.HIGHEST)
        product = product * active[None, :, None]
        return totals.at[:, col_ids, :].add(product)

    start_totals = jnp.zeros((rows_here, blocks.shape[1], tile_width), jnp.float32)
    return lax.fori_loop(0, groups, group_step, start_totals)


def dense_ladder(amplitudes, integrals, tile_rows, tile_cols, tile_count):
    rows_here = amplitudes.shape[0]
    columns_all = amplitudes.shape[1] * lax.axis_size("tile")
    gathered = lax.all_gather(amplitudes, "tile", axis=1, tiled=True)
    blocks = gathered.reshape(rows_here, columns_all // WIDTH, WIDTH)
    partial_value = contract(blocks, integrals, tile_rows, tile_cols, tile_count[0])
    partial_value = partial_value.reshape(rows_here, columns_all)
    return lax.psum_scatter(partial_value, "tile", scatter_dimension=1, tiled=True)


def home(row, col):
    return jnp.minimum(row, col) >> 6


class Part:
    def __init__(self, ref, first, width=0):
        self.ref, self.first, self.width = ref, first, width

    def spot(self, key):
        if isinstance(key, tuple):
            return self.first + key[0] * self.width + key[1]
        return self.first + key

    def __getitem__(self, key):
        return self.ref[self.spot(key)]

    def __setitem__(self, key, value):
        self.ref[self.spot(key)] = value


OWN_WIDTH = (XS + 1) * LIST
MOVED_WIDTH = 2 * LIST


def own_parts(ref):
    return Part(ref, 0), Part(ref, 8), Part(ref, 24, OWN_WIDTH)


def moved_parts(ref):
    return Part(ref, 0), Part(ref, 8, MOVED_WIDTH)


def pad_list(table, first, size, row, col):
    for pad in range(GROUP):
        table[0, first + size + pad] = 0
        table[1, first + size + pad] = row
        table[2, first + size + pad] = col


def pack_kernel(here, rows, cols, count, stored, *refs):
    outs, (plan, mine_of, entries, sems) = refs[:XS - 1], refs[XS - 1:]
    place, sizes, table = own_parts(plan)
    for each in range(3):
        place[each] = here[each]
    mine = place[0]
    low = mine * HERE
    fetch = pltpu.make_async_copy(stored.at[:, pl.ds(pl.multiple_of(place[1] * PIECE, PIECE), PIECE)], mine_of, sems.at[XS - 1])
    fetch.start()
    for each in range(8):
        sizes[each] = 0

    def sort_step(slot, _):
        row, col = rows[slot], cols[slot]
        target = (home(row, col) - mine) & (XS - 1)
        kind = jnp.where((target == 0) & (row - low >= HERE), XS, target)
        position = sizes[kind]
        at = kind * LIST + position
        table[0, at] = slot
        table[1, at] = row
        table[2, at] = col
        sizes[kind] = position + 1
        return 0

    lax.fori_loop(0, count[0], sort_step, 0)
    over = jnp.int32(0)
    for j in range(1, XS):
        over = jnp.maximum(over, (sizes[j] > CAP).astype(jnp.int32))
    sizes[XS + 1] = over
    fetch.wait()
    pad_list(table, 0, sizes[0], low, low + HERE + EXTRA)
    pad_list(table, XS * LIST, sizes[XS], low + HERE, low + HERE)
    copies = []
    for j in range(1, XS):
        out = outs[j - 1]
        entries[j - 1, 2, 0] = over.astype(jnp.float32)
        entries[j - 1, 3, mine] = 0.0
        for other in range(1, XS):
            entries[j - 1, 3, (mine + other) & (XS - 1)] = sizes[other].astype(jnp.float32)

        def move_step(item, _):
            at = j * LIST + item
            out[item] = mine_of[table[0, at]]
            entries[j - 1, 0, item] = table[1, at].astype(jnp.float32)
            entries[j - 1, 1, item] = table[2, at].astype(jnp.float32)
            return 0

        lax.fori_loop(0, jnp.minimum(sizes[j], CAP), move_step, 0)
        copy = pltpu.make_async_copy(entries.at[j - 1], out.at[CAP, pl.ds(0, 8)], sems.at[j - 1])
        copy.start()
        copies.append(copy)
    for copy in copies:
        copy.wait()


def pack(place, rows, cols, count, integrals):
    slots = integrals.shape[0]
    vmem = pl.BlockSpec(memory_space=pltpu.VMEM)
    smem = pl.BlockSpec(memory_space=pltpu.SMEM)
    return pl.pallas_call(
        pack_kernel,
        in_specs=[smem] * 4 + [pl.BlockSpec(memory_space=pl.ANY)],
        out_specs=[vmem] * (XS - 1) + [smem],
        out_shape=[jax.ShapeDtypeStruct((CAP + 1, PIECE, WIDTH), jnp.float32)] * (XS - 1)
        + [jax.ShapeDtypeStruct((24 + 3 * OWN_WIDTH,), jnp.int32)],
        scratch_shapes=[
            pltpu.VMEM((slots, PIECE, WIDTH), jnp.float32),
            pltpu.SMEM((XS - 1, 8, WIDTH), jnp.float32),
            pltpu.SemaphoreType.DMA((XS,)),
        ],
        compiler_params=pltpu.CompilerParams(vmem_limit_bytes=8 * 2**20),
        name="pack",
    )(place, rows, cols, count, integrals)


def compact_kernel(plan, *refs):
    sources, (out, moved_plan, entries, sems) = refs[:XS - 1], refs[XS - 1:]
    place, sizes, _ = own_parts(plan)
    totals, table = moved_parts(moved_plan)
    mine = place[0]
    low = mine * HERE
    copies = [
        pltpu.make_async_copy(sources[j].at[CAP, pl.ds(0, 8)], entries.at[j], sems.at[j]) for j in range(XS - 1)
    ]
    for copy in copies:
        copy.start()
    for copy in copies:
        copy.wait()
    for each in range(8):
        totals[each] = 0
    over = sizes[XS + 1] > 0
    for j in range(XS - 1):
        over = over | (entries[j, 2, 0] > 0.5)
    for j in range(XS):
        there = (mine + j) & (XS - 1)
        total = jnp.int32(0) if j == 0 else sizes[j]
        for source in range(XS - 1):
            total = total + entries[source, 3, there].astype(jnp.int32)
        over = over | (total > TOTAL_CAP)
    for j in range(XS - 1):
        source = sources[j]
        size = jnp.minimum(entries[j, 3, mine].astype(jnp.int32), CAP)

        def step(item, _):
            row = entries[j, 0, item].astype(jnp.int32)
            col = entries[j, 1, item].astype(jnp.int32)
            kind = jnp.where(row - low >= HERE, 1, 0)
            position = jnp.minimum(totals[kind], TOTAL_CAP - 1)
            out[jnp.where(kind == 1, TOTAL_CAP - 1 - position, position)] = source[item]
            at = kind * LIST + position
            table[1, at] = row
            table[2, at] = col
            totals[kind] = position + 1
            return 0

        lax.fori_loop(0, size, step, 0)
    totals[2] = over.astype(jnp.int32)
    pad_list(table, 0, totals[0], low, low + HERE + EXTRA)
    pad_list(table, LIST, totals[1], low + HERE, low + HERE)


def compact(plan, sources):
    vmem = pl.BlockSpec(memory_space=pltpu.VMEM)
    smem = pl.BlockSpec(memory_space=pltpu.SMEM)
    return pl.pallas_call(
        compact_kernel,
        in_specs=[smem] + [vmem] * (XS - 1),
        out_specs=[vmem, smem],
        out_shape=[
            jax.ShapeDtypeStruct((TOTAL_CAP, PIECE, WIDTH), jnp.float32),
            jax.ShapeDtypeStruct((8 + 3 * MOVED_WIDTH,), jnp.int32),
        ],
        scratch_shapes=[pltpu.SMEM((XS - 1, 8, WIDTH), jnp.float32), pltpu.SemaphoreType.DMA((XS - 1,))],
        compiler_params=pltpu.CompilerParams(vmem_limit_bytes=8 * 2**20),
        name="compact",
    )(plan, *sources)


def split_of(value):
    high = value.astype(jnp.bfloat16)
    return high, (value - high.astype(jnp.float32)).astype(jnp.bfloat16)


def products_of(low, table, first, size, left, fetch, sums):
    blank = jnp.zeros((WIDTH, WIDTH), jnp.bfloat16)

    def step(group, _):
        products = []
        for member in range(GROUP):
            item = group * GROUP + member
            high, rest = split_of(fetch(member, item, table[0, first + item]))
            right = jnp.concatenate(
                [jnp.concatenate([high, rest], axis=1), jnp.concatenate([high, blank], axis=1)], axis=0
            )
            product = jnp.dot(left(table[1, first + item] - low), right, preferred_element_type=jnp.float32)
            products.append(product[:, :WIDTH] + product[:, WIDTH:])
        for member in range(GROUP):
            col = table[2, first + group * GROUP + member] - low
            lanes = pl.ds(pl.multiple_of((col & (ZS - 1)) * WIDTH, WIDTH), WIDTH)
            sums[(col >> 3), :, lanes] += products[member]
        return 0

    lax.fori_loop(0, (size + GROUP - 1) >> 3, step, 0)


def split_at(source, row):
    lanes = pl.ds(pl.multiple_of((row & (ZS - 1)) * WIDTH, WIDTH), WIDTH)
    return jnp.concatenate(split_of(source[(row >> 3), :, lanes]), axis=1)


def start_own(table, first, size, stored_hbm, stored, sems):
    def step(item, _):
        pltpu.make_async_copy(stored_hbm.at[table[0, first + item]], stored.at[item], sems.at[item]).start()
        return 0

    lax.fori_loop(0, size, step, 0)


def wait_own(size, stored_hbm, stored, sems):
    def step(item, _):
        pltpu.make_async_copy(stored_hbm.at[0], stored.at[item], sems.at[item]).wait()
        return 0

    lax.fori_loop(0, size, step, 0)


def piece_rows(place):
    my_y = place[1] >> 1
    my_core = place[1] & 1
    rows = []
    for shift in range(YS):
        for swapped in range(2):
            core = my_core if swapped == 0 else 1 - my_core
            rows.append(pl.multiple_of((((my_y - shift) & (YS - 1)) * 2 + core) * PIECE, PIECE))
    return rows


def prepare_kernel(near_hbm, split_hbm, first_hbm, near, split, sems):
    copies = [pltpu.make_async_copy(near_hbm.at[z], near.at[z], sems.at[z]) for z in range(ZS)]
    for copy in copies:
        copy.start()
    backs = []
    for z in range(ZS):
        copies[z].wait()
        if z == 1:
            firsts = pltpu.make_async_copy(near.at[pl.ds(0, 2)], first_hbm, sems.at[ZS])
            firsts.start()
        for part in range(ZS):
            value = near[z, :, part * WIDTH:(part + 1) * WIDTH]
            split[z * ZS + part] = jnp.concatenate(split_of(value), axis=1)
        back = pltpu.make_async_copy(split.at[pl.ds(z * ZS, ZS)], split_hbm.at[pl.ds(z * ZS, ZS)], sems.at[ZS + 1 + z])
        back.start()
        backs.append(back)
    firsts.wait()
    for back in backs:
        back.wait()


def prepare(near):
    _, rows_here, wide = near.shape
    return pl.pallas_call(
        prepare_kernel,
        in_specs=[pl.BlockSpec(memory_space=pl.ANY)],
        out_specs=[pl.BlockSpec(memory_space=pl.ANY)] * 2,
        out_shape=[
            jax.ShapeDtypeStruct((HERE, rows_here, 2 * WIDTH), jnp.bfloat16),
            jax.ShapeDtypeStruct((2, rows_here, wide), jnp.float32),
        ],
        scratch_shapes=[
            pltpu.VMEM(near.shape, jnp.float32),
            pltpu.VMEM((HERE, rows_here, 2 * WIDTH), jnp.bfloat16),
            pltpu.SemaphoreType.DMA((2 * ZS + 1,)),
        ],
        compiler_params=pltpu.CompilerParams(vmem_limit_bytes=LIMIT * 2**20),
        name="prepare",
    )(near)


def chunk_copies(pieces_hbm, tiles, sems, rows_of, source, target, size):
    return [
        pltpu.make_async_copy(
            pieces_hbm[k].at[pl.ds(source, size)],
            tiles.at[pl.ds(target, size), pl.ds(rows_of[k], PIECE)],
            sems.at[target // ROUND, k],
        )
        for k in range(2 * YS)
    ]


def main_kernel(plan, moved_plan, split_hbm, stored_hbm, *refs):
    place, sizes, own = own_parts(plan)
    totals, moved = moved_parts(moved_plan)
    pieces_hbm, refs = refs[:2 * YS], refs[2 * YS:]
    out_hbm, soon_hbm, later_hbm, stored, tiles, sums, split, sems, own_sems, tile_sems = refs
    low = place[0] * HERE
    rows_of = piece_rows(place)
    copies = [
        pltpu.make_async_copy(split_hbm.at[pl.ds(z * ZS, ZS)], split.at[pl.ds(z * ZS, ZS)], sems.at[z])
        for z in range(ZS)
    ]
    for copy in copies:
        copy.start()
    start_own(own, 0, sizes[0], stored_hbm, stored, own_sems)
    chunks = []
    for first in range(0, TOTAL_CAP - ROUND + 1, ROUND):
        size = ROUND if first + 2 * ROUND <= TOTAL_CAP else TOTAL_CAP - first
        chunks.append((first, size, chunk_copies(pieces_hbm, tiles, tile_sems, rows_of, first, first, size)))
    for first, size, chunk in chunks:
        for copy in chunk:
            pl.when(totals[0] > first)(copy.start)
    sums[...] = jnp.zeros_like(sums)
    left = lambda row: split[row]
    for copy in copies:
        copy.wait()
    wait_own(sizes[0], stored_hbm, stored, own_sems)
    products_of(low, own, 0, sizes[0], left, lambda member, item, index: stored[item], sums)
    for first, size, chunk in chunks:
        for copy in chunk:
            pl.when(totals[0] > first)(copy.wait)
        here = jnp.clip(totals[0] - first, 0, size)
        products_of(low, moved, first, here, left, lambda member, item, index, first=first: tiles[first + item], sums)
    soon = jnp.where(place[2] == ZS // 2 + 1, 1, 0)
    last = ZS
    backs = [
        pltpu.make_async_copy(sums.at[ZS + soon], soon_hbm, sems.at[last]),
        pltpu.make_async_copy(sums.at[ZS + 1 - soon], later_hbm, sems.at[last + 1]),
    ]
    for z in range(ZS):
        block = (place[2] + z) & (ZS - 1)
        backs.append(pltpu.make_async_copy(sums.at[block], out_hbm.at[z], sems.at[last + 2 + z]))
    for back in backs:
        back.start()
    for back in backs:
        back.wait()


def late_kernel(plan, moved_plan, sums_in, extra_hbm, stored_hbm, *refs):
    place, sizes, own = own_parts(plan)
    totals, moved = moved_parts(moved_plan)
    pieces_hbm, refs = refs[:2 * YS], refs[2 * YS:]
    sums_hbm, extra, own_tiles, moved_tiles, sums, touched, sems, own_sems, moved_sems = refs
    low = place[0] * HERE
    rows_of = piece_rows(place)
    own_first = XS * LIST

    left = lambda row: split_at(extra, row - HERE)

    def start_round(turn):
        start_own(own, own_first + turn * ROUND, own_here(turn), stored_hbm, own_tiles, own_sems)
        base = jnp.maximum(TOTAL_CAP - ROUND * (turn + 1), 0)
        chunk = chunk_copies(pieces_hbm, moved_tiles, moved_sems, rows_of, base, 0, ROUND)
        for copy in chunk:
            pl.when(moved_here(turn) > 0)(copy.start)
        return base, chunk

    def finish_round(turn, base, chunk):
        wait_own(own_here(turn), stored_hbm, own_tiles, own_sems)
        products_of(
            low, own, own_first + turn * ROUND, own_here(turn), left, lambda member, item, index: own_tiles[item], sums
        )
        for copy in chunk:
            pl.when(moved_here(turn) > 0)(copy.wait)

        def fetch(member, item, index):
            return moved_tiles[jnp.maximum(TOTAL_CAP - 1 - turn * ROUND - item - base, 0)]

        products_of(low, moved, LIST + turn * ROUND, moved_here(turn), left, fetch, sums)

    def own_here(turn):
        return jnp.clip(sizes[XS] - turn * ROUND, 0, ROUND)

    def moved_here(turn):
        return jnp.clip(totals[1] - turn * ROUND, 0, ROUND)

    def whole_round(turn, _):
        finish_round(turn, *start_round(turn))
        return 0

    def touch(table, first, size):
        def one(item, _):
            touched[(table[2, first + item] - low) >> 3] = 1
            return 0

        lax.fori_loop(0, size, one, 0)

    def spot(z):
        return (z - place[2]) & (ZS - 1)


    @pl.when(sizes[XS] + totals[1] > 0)
    def _():
        first_round = start_round(0)
        copies = [pltpu.make_async_copy(extra_hbm.at[z], extra.at[z], sems.at[ZS + z]) for z in range(2)]
        for copy in copies:
            copy.start()
        for z in range(ZS):
            touched[z] = 0
        touch(own, own_first, sizes[XS])
        touch(moved, LIST, totals[1])
        inward = [pltpu.make_async_copy(sums_in.at[spot(z)], sums.at[z], sems.at[z]) for z in range(ZS)]
        outward = [pltpu.make_async_copy(sums.at[z], sums_hbm.at[spot(z)], sems.at[z]) for z in range(ZS)]
        for z in range(ZS):
            pl.when(touched[z] > 0)(inward[z].start)
        sums[ZS] = jnp.zeros(sums.shape[1:], jnp.float32)
        for copy in copies:
            copy.wait()
        for z in range(ZS):
            pl.when(touched[z] > 0)(inward[z].wait)
        finish_round(0, *first_round)
        rounds = (jnp.maximum(sizes[XS], totals[1]) + ROUND - 1) >> 4
        lax.fori_loop(1, rounds, whole_round, 0)
        for z in range(ZS):
            pl.when(touched[z] > 0)(outward[z].start)
        for z in range(ZS):
            pl.when(touched[z] > 0)(outward[z].wait)


def call(kernel, name, scalars, arrays, outs, scratch, aliases):
    smem = pl.BlockSpec(memory_space=pltpu.SMEM)
    anywhere = pl.BlockSpec(memory_space=pl.ANY)
    return pl.pallas_call(
        kernel,
        in_specs=[smem] * len(scalars) + [anywhere] * len(arrays),
        out_specs=[anywhere] * len(outs),
        out_shape=[jax.ShapeDtypeStruct(shape, jnp.float32) for shape in outs],
        input_output_aliases=aliases,
        scratch_shapes=scratch,
        cost_estimate=pl.CostEstimate(flops=10**6, bytes_accessed=10**4, transcendentals=0),
        compiler_params=pltpu.CompilerParams(vmem_limit_bytes=LIMIT * 2**20),
        name=name,
    )(*scalars, *arrays)


def main_sums(scalars, split, stored, pieces, wide):
    rows_here = split.shape[1]
    scratch = [
        pltpu.VMEM((LIST,) + stored.shape[1:], jnp.float32),
        pltpu.VMEM((TOTAL_CAP + GROUP, WIDTH, WIDTH), jnp.float32),
        pltpu.VMEM((ZS + 3, rows_here, wide), jnp.float32),
        pltpu.VMEM(split.shape, jnp.bfloat16),
        pltpu.SemaphoreType.DMA((2 * ZS + 2,)),
        pltpu.SemaphoreType.DMA((LIST,)),
        pltpu.SemaphoreType.DMA((TOTAL_CAP // ROUND + 1, 2 * YS)),
    ]
    outs = [(ZS, rows_here, wide)] + [(rows_here, wide)] * 2
    return call(main_kernel, "main", scalars, [split, stored, *pieces], outs, scratch, {})


def late_sums(scalars, sums, extra, stored, pieces):
    _, rows_here, wide = sums.shape
    scratch = [
        pltpu.VMEM(extra.shape, jnp.float32),
        pltpu.VMEM((ROUND + GROUP, WIDTH, WIDTH), jnp.float32),
        pltpu.VMEM((ROUND, WIDTH, WIDTH), jnp.float32),
        pltpu.VMEM((ZS + 1, rows_here, wide), jnp.float32),
        pltpu.SMEM((ZS,), jnp.int32),
        pltpu.SemaphoreType.DMA((ZS + 2,)),
        pltpu.SemaphoreType.DMA((ROUND,)),
        pltpu.SemaphoreType.DMA((1, 2 * YS)),
    ]
    return call(late_kernel, "late", scalars, [sums, extra, stored, *pieces], [sums.shape], scratch, {2: 0})[0]


def ring_sum(sums, more):
    half = ZS // 2
    middle = sums[half] + more(half)
    rows_here = middle.shape[0]
    up, down = middle[:rows_here // 2], middle[rows_here // 2:]
    for step in range(half - 1, -1, -1):
        up, down = lax.optimization_barrier((up, down))
        up = lax.ppermute(up, "tile", z_shift(1))
        down = lax.ppermute(down, "tile", z_shift(-1))
        up, down = lax.optimization_barrier((up, down))
        if step == half - 1:
            up = jnp.concatenate([up, jnp.zeros_like(up)], axis=0)
            down = jnp.concatenate([jnp.zeros_like(down), down], axis=0)
        if step > 0:
            up = up + (sums[step] + more(step))
            down = down + (sums[ZS - step] + more(ZS - step))
    return sums[0] + more(0) + up + down


def shards(
    amplitudes, driver, integrals, tile_rows, tile_cols, tile_count, pair_energy, virt_energy
):
    my_tile = lax.axis_index("tile")
    my_x = my_tile // ZS
    my_z = lax.rem(my_tile, ZS)
    place = jnp.stack([my_x, lax.axis_index("pair"), my_z]).astype(jnp.int32)

    near = lax.all_gather(amplitudes, "tile", axis=0, axis_index_groups=Z_GROUPS)

    *packed, plan = pack(place, tile_rows, tile_cols, tile_count, integrals)
    arrived = [lax.ppermute(packed[step - 1], "tile", x_shift(step)) for step in range(1, XS)]
    mine, moved_plan = compact(plan, arrived)
    along_y = [mine] + [lax.ppermute(mine, "pair", y_shift(step)) for step in range(1, YS)]
    across = lax.ppermute(mine, "pair", CORE_SWAP)
    marks = moved_plan[2:3].astype(jnp.float32)
    for step in (1, 2, 4):
        marks = jnp.maximum(marks, lax.ppermute(marks, "tile", z_shift(step)))
    split, first = prepare(near)
    extra = lax.ppermute(first, "tile", x_shift(-1))
    along_y[1], along_y[2], first, marks = lax.optimization_barrier((along_y[1], along_y[2], first, marks))
    pieces = [mine, across]
    for piece in along_y[1:]:
        pieces += [piece, lax.ppermute(piece, "pair", CORE_SWAP)]
    scalars = (plan, moved_plan)
    sums, soon, later = main_sums(scalars, split, integrals, pieces, near.shape[2])
    soon = lax.ppermute(soon, "tile", x_shift(1))
    later = lax.ppermute(later, "tile", x_shift(1))
    sums = late_sums(scalars, sums, extra, integrals, pieces)
    soon_block = jnp.where(my_z == ZS // 2 + 1, 1, 0)

    def more(step):
        block = lax.rem(my_z + step, ZS)
        value = jnp.where(block == soon_block, soon, 0.0)
        if step == ZS // 2:
            return value
        return jnp.where(block == 1 - soon_block, later, value)

    ladder = ring_sum(sums, more)
    denominator = virt_energy[None, :] - pair_energy[:, None]
    result = (driver + ladder) / denominator

    def slow():
        full = dense_ladder(amplitudes, integrals, tile_rows, tile_cols, tile_count)
        return (driver + full) / denominator

    return lax.cond(marks[0] > 0.5, slow, lambda: result)


def solution(mesh):
    return jax.shard_map(
        shards,
        mesh=mesh,
        in_specs=(
            P("pair", "tile"),
            P("pair", "tile"),
            P("tile", None, None),
            P("tile"),
            P("tile"),
            P("tile"),
            P("pair"),
            P("tile"),
        ),
        out_specs=P("pair", "tile"),
        check_vma=False,
    )
```

```python
import jax
import jax.numpy as jnp
from jax import lax
from jax.experimental import pallas as pl
from jax.experimental.pallas import tpu as pltpu
from jax.sharding import PartitionSpec as P

XS = 4
ZS = 8
YS = 4
CAP = 32
TOTAL_CAP = 64
LIST = 72
GROUP = 8
EXTRA = 16
ROUND = 16
LIMIT = 53
HERE = 64
PIECE = 16
WIDTH = 128

Z_GROUPS = [[x * ZS + z for z in range(ZS)] for x in range(XS)]


def x_shift(step):
    return [(x * ZS + z, ((x + step) % XS) * ZS + z) for x in range(XS) for z in range(ZS)]


def z_shift(step):
    return [(x * ZS + z, x * ZS + (z + step) % ZS) for x in range(XS) for z in range(ZS)]


def y_shift(step):
    return [(y * 2 + core, ((y + step) % YS) * 2 + core) for y in range(YS) for core in range(2)]


CORE_SWAP = [(y * 2 + core, y * 2 + 1 - core) for y in range(YS) for core in range(2)]


def contract(blocks, stored, row_list, col_list, live_count):
    tile_width = stored.shape[1]
    group_size = 8
    slot_total = stored.shape[0]
    rows_here = blocks.shape[0]
    groups = (live_count + group_size - 1) // group_size

    def group_step(group, totals):
        index_list = group * group_size + jnp.arange(group_size, dtype=jnp.int32)
        safe_index = jnp.minimum(index_list, slot_total - 1)
        pieces = jnp.take(stored, safe_index, axis=0)
        row_ids = jnp.take(row_list, safe_index, axis=0)
        col_ids = jnp.take(col_list, safe_index, axis=0)
        active = (index_list < live_count).astype(jnp.float32)
        inputs = jnp.take(blocks, row_ids, axis=1)
        product = jnp.einsum("pgk,gkn->pgn", inputs, pieces, precision=lax.Precision.HIGHEST)
        product = product * active[None, :, None]
        return totals.at[:, col_ids, :].add(product)

    start_totals = jnp.zeros((rows_here, blocks.shape[1], tile_width), jnp.float32)
    return lax.fori_loop(0, groups, group_step, start_totals)


def dense_ladder(amplitudes, integrals, tile_rows, tile_cols, tile_count):
    rows_here = amplitudes.shape[0]
    columns_all = amplitudes.shape[1] * lax.axis_size("tile")
    gathered = lax.all_gather(amplitudes, "tile", axis=1, tiled=True)
    blocks = gathered.reshape(rows_here, columns_all // WIDTH, WIDTH)
    partial_value = contract(blocks, integrals, tile_rows, tile_cols, tile_count[0])
    partial_value = partial_value.reshape(rows_here, columns_all)
    return lax.psum_scatter(partial_value, "tile", scatter_dimension=1, tiled=True)


def home(row, col):
    return jnp.minimum(row, col) >> 6


class Part:
    def __init__(self, ref, first, width=0):
        self.ref, self.first, self.width = ref, first, width

    def spot(self, key):
        if isinstance(key, tuple):
            return self.first + key[0] * self.width + key[1]
        return self.first + key

    def __getitem__(self, key):
        return self.ref[self.spot(key)]

    def __setitem__(self, key, value):
        self.ref[self.spot(key)] = value


OWN_WIDTH = (XS + 1) * LIST
MOVED_WIDTH = 2 * LIST


def own_parts(ref):
    return Part(ref, 0), Part(ref, 8), Part(ref, 24, OWN_WIDTH)


def moved_parts(ref):
    return Part(ref, 0), Part(ref, 8, MOVED_WIDTH)


def pad_list(table, first, size, row, col):
    for pad in range(GROUP):
        table[0, first + size + pad] = 0
        table[1, first + size + pad] = row
        table[2, first + size + pad] = col


def pack_kernel(here, rows, cols, count, stored, *refs):
    outs, (plan, mine_of, entries, sems) = refs[:XS - 1], refs[XS - 1:]
    place, sizes, table = own_parts(plan)
    for each in range(3):
        place[each] = here[each]
    mine = place[0]
    low = mine * HERE
    fetch = pltpu.make_async_copy(stored.at[:, pl.ds(pl.multiple_of(place[1] * PIECE, PIECE), PIECE)], mine_of, sems.at[XS - 1])
    fetch.start()
    for each in range(8):
        sizes[each] = 0

    def sort_step(slot, _):
        row, col = rows[slot], cols[slot]
        target = (home(row, col) - mine) & (XS - 1)
        kind = jnp.where((target == 0) & (row - low >= HERE), XS, target)
        position = sizes[kind]
        at = kind * LIST + position
        table[0, at] = slot
        table[1, at] = row
        table[2, at] = col
        sizes[kind] = position + 1
        return 0

    lax.fori_loop(0, count[0], sort_step, 0)
    over = jnp.int32(0)
    for j in range(1, XS):
        over = jnp.maximum(over, (sizes[j] > CAP).astype(jnp.int32))
    sizes[XS + 1] = over
    fetch.wait()
    pad_list(table, 0, sizes[0], low, low + HERE + EXTRA)
    pad_list(table, XS * LIST, sizes[XS], low + HERE, low + HERE)
    copies = []
    for j in range(1, XS):
        out = outs[j - 1]
        entries[j - 1, 2, 0] = over.astype(jnp.float32)
        entries[j - 1, 3, mine] = 0.0
        for other in range(1, XS):
            entries[j - 1, 3, (mine + other) & (XS - 1)] = sizes[other].astype(jnp.float32)

        def move_step(item, _):
            at = j * LIST + item
            out[item] = mine_of[table[0, at]]
            entries[j - 1, 0, item] = table[1, at].astype(jnp.float32)
            entries[j - 1, 1, item] = table[2, at].astype(jnp.float32)
            return 0

        lax.fori_loop(0, jnp.minimum(sizes[j], CAP), move_step, 0)
        copy = pltpu.make_async_copy(entries.at[j - 1], out.at[CAP, pl.ds(0, 8)], sems.at[j - 1])
        copy.start()
        copies.append(copy)
    for copy in copies:
        copy.wait()


def pack(place, rows, cols, count, integrals):
    slots = integrals.shape[0]
    vmem = pl.BlockSpec(memory_space=pltpu.VMEM)
    smem = pl.BlockSpec(memory_space=pltpu.SMEM)
    return pl.pallas_call(
        pack_kernel,
        in_specs=[smem] * 4 + [pl.BlockSpec(memory_space=pl.ANY)],
        out_specs=[vmem] * (XS - 1) + [smem],
        out_shape=[jax.ShapeDtypeStruct((CAP + 1, PIECE, WIDTH), jnp.float32)] * (XS - 1)
        + [jax.ShapeDtypeStruct((24 + 3 * OWN_WIDTH,), jnp.int32)],
        scratch_shapes=[
            pltpu.VMEM((slots, PIECE, WIDTH), jnp.float32),
            pltpu.SMEM((XS - 1, 8, WIDTH), jnp.float32),
            pltpu.SemaphoreType.DMA((XS,)),
        ],
        compiler_params=pltpu.CompilerParams(vmem_limit_bytes=8 * 2**20),
        name="pack",
    )(place, rows, cols, count, integrals)


def compact_kernel(plan, *refs):
    sources, (out, moved_plan, mark, entries, sems) = refs[:XS - 1], refs[XS - 1:]
    place, sizes, _ = own_parts(plan)
    totals, table = moved_parts(moved_plan)
    mine = place[0]
    low = mine * HERE
    copies = [
        pltpu.make_async_copy(sources[j].at[CAP, pl.ds(0, 8)], entries.at[j], sems.at[j]) for j in range(XS - 1)
    ]
    for copy in copies:
        copy.start()
    for copy in copies:
        copy.wait()
    for each in range(8):
        totals[each] = 0
    over = sizes[XS + 1] > 0
    for j in range(XS - 1):
        over = over | (entries[j, 2, 0] > 0.5)
    for j in range(XS):
        there = (mine + j) & (XS - 1)
        total = jnp.int32(0) if j == 0 else sizes[j]
        for source in range(XS - 1):
            total = total + entries[source, 3, there].astype(jnp.int32)
        over = over | (total > TOTAL_CAP)
    for j in range(XS - 1):
        source = sources[j]
        size = jnp.minimum(entries[j, 3, mine].astype(jnp.int32), CAP)

        def step(item, _):
            row = entries[j, 0, item].astype(jnp.int32)
            col = entries[j, 1, item].astype(jnp.int32)
            kind = jnp.where(row - low >= HERE, 1, 0)
            position = jnp.minimum(totals[kind], TOTAL_CAP - 1)
            out[jnp.where(kind == 1, TOTAL_CAP - 1 - position, position)] = source[item]
            at = kind * LIST + position
            table[1, at] = row
            table[2, at] = col
            totals[kind] = position + 1
            return 0

        lax.fori_loop(0, size, step, 0)
    mark[...] = jnp.broadcast_to(over.astype(jnp.float32), mark.shape)
    pad_list(table, 0, totals[0], low, low + HERE + EXTRA)
    pad_list(table, LIST, totals[1], low + HERE, low + HERE)


def compact(plan, sources):
    vmem = pl.BlockSpec(memory_space=pltpu.VMEM)
    smem = pl.BlockSpec(memory_space=pltpu.SMEM)
    return pl.pallas_call(
        compact_kernel,
        in_specs=[smem] + [vmem] * (XS - 1),
        out_specs=[vmem, smem, vmem],
        out_shape=[
            jax.ShapeDtypeStruct((TOTAL_CAP, PIECE, WIDTH), jnp.float32),
            jax.ShapeDtypeStruct((8 + 3 * MOVED_WIDTH,), jnp.int32),
            jax.ShapeDtypeStruct((8, WIDTH), jnp.float32),
        ],
        scratch_shapes=[pltpu.SMEM((XS - 1, 8, WIDTH), jnp.float32), pltpu.SemaphoreType.DMA((XS - 1,))],
        compiler_params=pltpu.CompilerParams(vmem_limit_bytes=8 * 2**20),
        name="compact",
    )(plan, *sources)


def split_of(value):
    high = value.astype(jnp.bfloat16)
    return high, (value - high.astype(jnp.float32)).astype(jnp.bfloat16)


def products_of(low, table, first, size, left, fetch, sums):
    blank = jnp.zeros((WIDTH, WIDTH), jnp.bfloat16)

    def step(group, _):
        products = []
        for member in range(GROUP):
            item = group * GROUP + member
            high, rest = split_of(fetch(member, item, table[0, first + item]))
            right = jnp.concatenate(
                [jnp.concatenate([high, rest], axis=1), jnp.concatenate([high, blank], axis=1)], axis=0
            )
            product = jnp.dot(left(table[1, first + item] - low), right, preferred_element_type=jnp.float32)
            products.append(product[:, :WIDTH] + product[:, WIDTH:])
        for member in range(GROUP):
            col = table[2, first + group * GROUP + member] - low
            lanes = pl.ds(pl.multiple_of((col & (ZS - 1)) * WIDTH, WIDTH), WIDTH)
            sums[(col >> 3), :, lanes] += products[member]
        return 0

    lax.fori_loop(0, (size + GROUP - 1) >> 3, step, 0)


def split_at(source, row):
    lanes = pl.ds(pl.multiple_of((row & (ZS - 1)) * WIDTH, WIDTH), WIDTH)
    return jnp.concatenate(split_of(source[(row >> 3), :, lanes]), axis=1)


def start_own(table, first, size, stored_hbm, stored, sems):
    def step(item, _):
        pltpu.make_async_copy(stored_hbm.at[table[0, first + item]], stored.at[item], sems.at[item]).start()
        return 0

    lax.fori_loop(0, size, step, 0)


def wait_own(size, stored_hbm, stored, sems):
    def step(item, _):
        pltpu.make_async_copy(stored_hbm.at[0], stored.at[item], sems.at[item]).wait()
        return 0

    lax.fori_loop(0, size, step, 0)


def piece_rows(place):
    my_y = place[1] >> 1
    my_core = place[1] & 1
    rows = []
    for shift in range(YS):
        for swapped in range(2):
            core = my_core if swapped == 0 else 1 - my_core
            rows.append(pl.multiple_of((((my_y - shift) & (YS - 1)) * 2 + core) * PIECE, PIECE))
    return rows


def prepare_kernel(near_hbm, split_hbm, first_hbm, near, split, sems):
    copies = [pltpu.make_async_copy(near_hbm.at[z], near.at[z], sems.at[z]) for z in range(ZS)]
    for copy in copies:
        copy.start()
    backs = []
    for z in range(ZS):
        copies[z].wait()
        if z == 1:
            firsts = pltpu.make_async_copy(near.at[pl.ds(0, 2)], first_hbm, sems.at[ZS])
            firsts.start()
        for part in range(ZS):
            value = near[z, :, part * WIDTH:(part + 1) * WIDTH]
            split[z * ZS + part] = jnp.concatenate(split_of(value), axis=1)
        back = pltpu.make_async_copy(split.at[pl.ds(z * ZS, ZS)], split_hbm.at[pl.ds(z * ZS, ZS)], sems.at[ZS + 1 + z])
        back.start()
        backs.append(back)
    firsts.wait()
    for back in backs:
        back.wait()


def prepare(near):
    _, rows_here, wide = near.shape
    return pl.pallas_call(
        prepare_kernel,
        in_specs=[pl.BlockSpec(memory_space=pl.ANY)],
        out_specs=[pl.BlockSpec(memory_space=pl.ANY)] * 2,
        out_shape=[
            jax.ShapeDtypeStruct((HERE, rows_here, 2 * WIDTH), jnp.bfloat16),
            jax.ShapeDtypeStruct((2, rows_here, wide), jnp.float32),
        ],
        scratch_shapes=[
            pltpu.VMEM(near.shape, jnp.float32),
            pltpu.VMEM((HERE, rows_here, 2 * WIDTH), jnp.bfloat16),
            pltpu.SemaphoreType.DMA((2 * ZS + 1,)),
        ],
        compiler_params=pltpu.CompilerParams(vmem_limit_bytes=LIMIT * 2**20),
        name="prepare",
    )(near)


def chunk_copies(pieces_hbm, tiles, sems, rows_of, source, target, size):
    return [
        pltpu.make_async_copy(
            pieces_hbm[k].at[pl.ds(source, size)],
            tiles.at[pl.ds(target, size), pl.ds(rows_of[k], PIECE)],
            sems.at[target // ROUND, k],
        )
        for k in range(2 * YS)
    ]


def main_kernel(plan, moved_plan, split_hbm, stored_hbm, *refs):
    place, sizes, own = own_parts(plan)
    totals, moved = moved_parts(moved_plan)
    pieces_hbm, refs = refs[:2 * YS], refs[2 * YS:]
    out_hbm, soon_hbm, later_hbm, stored, tiles, sums, split, sems, own_sems, tile_sems = refs
    low = place[0] * HERE
    rows_of = piece_rows(place)
    copies = [
        pltpu.make_async_copy(split_hbm.at[pl.ds(z * ZS, ZS)], split.at[pl.ds(z * ZS, ZS)], sems.at[z])
        for z in range(ZS)
    ]
    for copy in copies:
        copy.start()
    start_own(own, 0, sizes[0], stored_hbm, stored, own_sems)
    chunks = []
    for first in range(0, TOTAL_CAP - ROUND + 1, ROUND):
        size = ROUND if first + 2 * ROUND <= TOTAL_CAP else TOTAL_CAP - first
        chunks.append((first, size, chunk_copies(pieces_hbm, tiles, tile_sems, rows_of, first, first, size)))
    for first, size, chunk in chunks:
        for copy in chunk:
            pl.when(totals[0] > first)(copy.start)
    sums[...] = jnp.zeros_like(sums)
    left = lambda row: split[row]
    for copy in copies:
        copy.wait()
    wait_own(sizes[0], stored_hbm, stored, own_sems)
    products_of(low, own, 0, sizes[0], left, lambda member, item, index: stored[item], sums)
    for first, size, chunk in chunks:
        for copy in chunk:
            pl.when(totals[0] > first)(copy.wait)
        here = jnp.clip(totals[0] - first, 0, size)
        products_of(low, moved, first, here, left, lambda member, item, index, first=first: tiles[first + item], sums)
    soon = jnp.where(place[2] == ZS // 2 + 1, 1, 0)
    last = ZS
    backs = [
        pltpu.make_async_copy(sums.at[ZS + soon], soon_hbm, sems.at[last]),
        pltpu.make_async_copy(sums.at[ZS + 1 - soon], later_hbm, sems.at[last + 1]),
    ]
    for z in range(ZS):
        block = (place[2] + z) & (ZS - 1)
        backs.append(pltpu.make_async_copy(sums.at[block], out_hbm.at[z], sems.at[last + 2 + z]))
    for back in backs:
        back.start()
    for back in backs:
        back.wait()


def late_kernel(plan, moved_plan, sums_in, extra_hbm, stored_hbm, *refs):
    place, sizes, own = own_parts(plan)
    totals, moved = moved_parts(moved_plan)
    pieces_hbm, refs = refs[:2 * YS], refs[2 * YS:]
    sums_hbm, extra, own_tiles, moved_tiles, sums, touched, sems, own_sems, moved_sems = refs
    low = place[0] * HERE
    rows_of = piece_rows(place)
    own_first = XS * LIST

    left = lambda row: split_at(extra, row - HERE)

    def start_round(turn):
        start_own(own, own_first + turn * ROUND, own_here(turn), stored_hbm, own_tiles, own_sems)
        base = jnp.maximum(TOTAL_CAP - ROUND * (turn + 1), 0)
        chunk = chunk_copies(pieces_hbm, moved_tiles, moved_sems, rows_of, base, 0, ROUND)
        for copy in chunk:
            pl.when(moved_here(turn) > 0)(copy.start)
        return base, chunk

    def finish_round(turn, base, chunk):
        wait_own(own_here(turn), stored_hbm, own_tiles, own_sems)
        products_of(
            low, own, own_first + turn * ROUND, own_here(turn), left, lambda member, item, index: own_tiles[item], sums
        )
        for copy in chunk:
            pl.when(moved_here(turn) > 0)(copy.wait)

        def fetch(member, item, index):
            return moved_tiles[jnp.maximum(TOTAL_CAP - 1 - turn * ROUND - item - base, 0)]

        products_of(low, moved, LIST + turn * ROUND, moved_here(turn), left, fetch, sums)

    def own_here(turn):
        return jnp.clip(sizes[XS] - turn * ROUND, 0, ROUND)

    def moved_here(turn):
        return jnp.clip(totals[1] - turn * ROUND, 0, ROUND)

    def whole_round(turn, _):
        finish_round(turn, *start_round(turn))
        return 0

    def touch(table, first, size):
        def one(item, _):
            touched[(table[2, first + item] - low) >> 3] = 1
            return 0

        lax.fori_loop(0, size, one, 0)

    def spot(z):
        return (z - place[2]) & (ZS - 1)


    @pl.when(sizes[XS] + totals[1] > 0)
    def _():
        first_round = start_round(0)
        copies = [pltpu.make_async_copy(extra_hbm.at[z], extra.at[z], sems.at[ZS + z]) for z in range(2)]
        for copy in copies:
            copy.start()
        for z in range(ZS):
            touched[z] = 0
        touch(own, own_first, sizes[XS])
        touch(moved, LIST, totals[1])
        inward = [pltpu.make_async_copy(sums_in.at[spot(z)], sums.at[z], sems.at[z]) for z in range(ZS)]
        outward = [pltpu.make_async_copy(sums.at[z], sums_hbm.at[spot(z)], sems.at[z]) for z in range(ZS)]
        for z in range(ZS):
            pl.when(touched[z] > 0)(inward[z].start)
        sums[ZS] = jnp.zeros(sums.shape[1:], jnp.float32)
        for copy in copies:
            copy.wait()
        for z in range(ZS):
            pl.when(touched[z] > 0)(inward[z].wait)
        finish_round(0, *first_round)
        rounds = (jnp.maximum(sizes[XS], totals[1]) + ROUND - 1) >> 4
        lax.fori_loop(1, rounds, whole_round, 0)
        for z in range(ZS):
            pl.when(touched[z] > 0)(outward[z].start)
        for z in range(ZS):
            pl.when(touched[z] > 0)(outward[z].wait)


def call(kernel, name, scalars, arrays, outs, scratch, aliases):
    smem = pl.BlockSpec(memory_space=pltpu.SMEM)
    anywhere = pl.BlockSpec(memory_space=pl.ANY)
    return pl.pallas_call(
        kernel,
        in_specs=[smem] * len(scalars) + [anywhere] * len(arrays),
        out_specs=[anywhere] * len(outs),
        out_shape=[jax.ShapeDtypeStruct(shape, jnp.float32) for shape in outs],
        input_output_aliases=aliases,
        scratch_shapes=scratch,
        cost_estimate=pl.CostEstimate(flops=10**6, bytes_accessed=10**4, transcendentals=0),
        compiler_params=pltpu.CompilerParams(vmem_limit_bytes=LIMIT * 2**20),
        name=name,
    )(*scalars, *arrays)


def main_sums(scalars, split, stored, pieces, wide):
    rows_here = split.shape[1]
    scratch = [
        pltpu.VMEM((LIST,) + stored.shape[1:], jnp.float32),
        pltpu.VMEM((TOTAL_CAP + GROUP, WIDTH, WIDTH), jnp.float32),
        pltpu.VMEM((ZS + 3, rows_here, wide), jnp.float32),
        pltpu.VMEM(split.shape, jnp.bfloat16),
        pltpu.SemaphoreType.DMA((2 * ZS + 2,)),
        pltpu.SemaphoreType.DMA((LIST,)),
        pltpu.SemaphoreType.DMA((TOTAL_CAP // ROUND + 1, 2 * YS)),
    ]
    outs = [(ZS, rows_here, wide)] + [(rows_here, wide)] * 2
    return call(main_kernel, "main", scalars, [split, stored, *pieces], outs, scratch, {})


def late_sums(scalars, sums, extra, stored, pieces):
    _, rows_here, wide = sums.shape
    scratch = [
        pltpu.VMEM(extra.shape, jnp.float32),
        pltpu.VMEM((ROUND + GROUP, WIDTH, WIDTH), jnp.float32),
        pltpu.VMEM((ROUND, WIDTH, WIDTH), jnp.float32),
        pltpu.VMEM((ZS + 1, rows_here, wide), jnp.float32),
        pltpu.SMEM((ZS,), jnp.int32),
        pltpu.SemaphoreType.DMA((ZS + 2,)),
        pltpu.SemaphoreType.DMA((ROUND,)),
        pltpu.SemaphoreType.DMA((1, 2 * YS)),
    ]
    return call(late_kernel, "late", scalars, [sums, extra, stored, *pieces], [sums.shape], scratch, {2: 0})[0]


def ring_sum(sums, more):
    half = ZS // 2
    middle = sums[half] + more(half)
    rows_here = middle.shape[0]
    up, down = middle[:rows_here // 2], middle[rows_here // 2:]
    for step in range(half - 1, -1, -1):
        up, down = lax.optimization_barrier((up, down))
        up = lax.ppermute(up, "tile", z_shift(1))
        down = lax.ppermute(down, "tile", z_shift(-1))
        up, down = lax.optimization_barrier((up, down))
        if step == half - 1:
            up = jnp.concatenate([up, jnp.zeros_like(up)], axis=0)
            down = jnp.concatenate([jnp.zeros_like(down), down], axis=0)
        if step > 0:
            up = up + (sums[step] + more(step))
            down = down + (sums[ZS - step] + more(ZS - step))
    return sums[0] + more(0) + up + down


def shards(
    amplitudes, driver, integrals, tile_rows, tile_cols, tile_count, pair_energy, virt_energy
):
    my_tile = lax.axis_index("tile")
    my_x = my_tile // ZS
    my_z = lax.rem(my_tile, ZS)
    place = jnp.stack([my_x, lax.axis_index("pair"), my_z]).astype(jnp.int32)

    near = lax.all_gather(amplitudes, "tile", axis=0, axis_index_groups=Z_GROUPS)

    *packed, plan = pack(place, tile_rows, tile_cols, tile_count, integrals)
    arrived = [lax.ppermute(packed[step - 1], "tile", x_shift(step)) for step in (2, 1, 3)]
    mine, moved_plan, marks = compact(plan, arrived)
    along_y = [mine] + [lax.ppermute(mine, "pair", y_shift(step)) for step in range(1, YS)]
    across = lax.ppermute(mine, "pair", CORE_SWAP)
    for step in (1, 2, 4):
        marks = jnp.maximum(marks, lax.ppermute(marks, "tile", z_shift(step)))
    split, first = prepare(near)
    extra = lax.ppermute(first, "tile", x_shift(-1))
    along_y[1], along_y[2], marks = lax.optimization_barrier((along_y[1], along_y[2], marks))
    pieces = [mine, across]
    for piece in along_y[1:]:
        pieces += [piece, lax.ppermute(piece, "pair", CORE_SWAP)]
    scalars = (plan, moved_plan)
    sums, soon, later = main_sums(scalars, split, integrals, pieces, near.shape[2])
    soon = lax.ppermute(soon, "tile", x_shift(1))
    later = lax.ppermute(later, "tile", x_shift(1))
    sums = late_sums(scalars, sums, extra, integrals, pieces)
    soon_block = jnp.where(my_z == ZS // 2 + 1, 1, 0)

    def more(step):
        block = lax.rem(my_z + step, ZS)
        value = jnp.where(block == soon_block, soon, 0.0)
        if step == ZS // 2:
            return value
        return jnp.where(block == 1 - soon_block, later, value)

    ladder = ring_sum(sums, more)
    denominator = virt_energy[None, :] - pair_energy[:, None]
    result = (driver + ladder) / denominator

    def slow():
        full = dense_ladder(amplitudes, integrals, tile_rows, tile_cols, tile_count)
        return (driver + full) / denominator

    return lax.cond(marks[0, 0] > 0.5, slow, lambda: result)


def solution(mesh):
    return jax.shard_map(
        shards,
        mesh=mesh,
        in_specs=(
            P("pair", "tile"),
            P("pair", "tile"),
            P("tile", None, None),
            P("tile"),
            P("tile"),
            P("tile"),
            P("pair"),
            P("tile"),
        ),
        out_specs=P("pair", "tile"),
        check_vma=False,
    )
```
